32 devices in a mesh: row: 4 (over y, core), col: 8 (over z, x).
Axes of the slice: x: 2, y: 2, z: 4, core: 2. Of those that a mesh axis runs over, the one named last changes fastest.
Arguments:
- block_values: bfloat16 [4, 8, 24, 256, 256], P('row', 'col'), may hold values from -0.078125 to 0.078125
- block_rows: int32 [4, 8, 24], P('row', 'col'), may hold values from 0 to 7, as said below
- block_cols: int32 [4, 8, 24], P('row', 'col'), may hold values from 0 to 7
- block_count: int32 [4, 8], P('row', 'col'), may hold values from 8 to 24, as said below
- basis: bfloat16 [16384, 256], P(('col', 'row')), may hold values from -6 to 6
Outputs:
- sweep_out: float32 [16384, 256], P(('col', 'row'))
The draws below stay inside these ranges and needn't reach their ends.
Inputs may be any that keep to these rules, and one draw needn't show every extreme that they name: Within one device all slots give distinct (block_rows, block_cols) pairs; slots at or beyond block_count hold no block. `block_count`: some device holds exactly 24 live slots.
All inputs are finite; a program needn't handle non-finite values.
Results may differ from the reference program's by a relative error of at most 0.0026.
Values may be sent and summed in bfloat16 or wider, within the bound.
A program may use at most 64 MiB of HBM per device.

```python
import jax
import jax.numpy as jnp
from jax import lax

BS = 256
RANK = 256
RB = 8
CB = 8
BMAX = 24
COLS = 16384
N_ROW = 4
N_COL = 8


def block_pattern(key):
    base = jax.random.fold_in(key, 11)
    perm_key, count_key, pick_key, top_key = jax.random.split(base, 4)
    device_total = N_ROW * N_COL
    keys = jax.random.split(perm_key, device_total)
    orders = jax.vmap(lambda one_key: jax.random.permutation(one_key, RB * CB))(keys)[:, :BMAX]
    lowest = max(1, BMAX // 3)
    spread = BMAX - lowest
    first = jax.random.randint(count_key, (device_total,), 0, spread + 1)
    second = jax.random.randint(pick_key, (device_total,), 0, spread + 1)
    counts = lowest + first * second // max(spread, 1)
    busiest = jax.random.randint(top_key, (), 0, device_total)
    counts = jnp.where(jnp.arange(device_total) == busiest, BMAX, counts)
    return (orders.astype(jnp.int32).reshape(N_ROW, N_COL, BMAX), counts.astype(jnp.int32).reshape(N_ROW, N_COL))


def draw_block_rows(key, part):
    orders, counts = block_pattern(key)
    return (orders // CB).astype(jnp.int32)


def draw_block_cols(key, part):
    orders, counts = block_pattern(key)
    return (orders % CB).astype(jnp.int32)


def draw_block_count(key, part):
    orders, counts = block_pattern(key)
    return counts


def shard_levels(stream_key, shape, cuts, smallest, top_value):
    def one(dim, parts):
        draws = jax.random.uniform(jax.random.fold_in(jax.random.fold_in(stream_key, 6), dim), (parts,), jnp.float32, smallest / len(cuts), top_value / len(cuts))
        return jnp.repeat(jnp.exp(draws), shape[dim] // parts).reshape((-1,) + (1,) * (len(shape) - dim - 1))

    gain = one(*cuts[0])
    for cut in cuts[1:]:
        gain = gain * one(*cut)
    return gain


def noise(own_key, dims, scale, reach, cuts=(), kind=jnp.bfloat16):
    entries = jax.random.normal(own_key, dims, jnp.float32) * scale
    if len(cuts) > 0:
        entries = shard_levels(own_key, dims, cuts, -0.22, 0.18) * entries
    return jnp.clip(entries, min=-reach, max=reach).astype(kind)


def setup_inputs(seed: int = 0) -> dict:
    streams_of = jax.random.split(jax.random.key(seed), 6)
    return {
        "block_values": noise(streams_of[0], (N_ROW, N_COL, BMAX, BS, BS), (BS * BMAX) ** -0.5, 0.078125, ((0, 4), (1, 8))),
        "block_rows": draw_block_rows(jax.random.fold_in(streams_of[5], 71), 0),
        "block_cols": draw_block_cols(jax.random.fold_in(streams_of[5], 71), 0),
        "block_count": draw_block_count(jax.random.fold_in(streams_of[5], 71), 0),
        "basis": noise(streams_of[4], (COLS, RANK), 1.0, 6.0, ((0, 32),)),
    }


def sweep(tiles, total_out, all_blocks, source_ids, target_ids, all_counts, forward):
    device_total = N_ROW * N_COL
    device_ids = jnp.arange(device_total, dtype=jnp.int32)
    slot_index = jnp.arange(BMAX, dtype=jnp.int32)
    if forward:
        in_count, out_count, form = CB, RB, "bij,bjk->bik"
    else:
        in_count, out_count, form = RB, CB, "bji,bjk->bik"

    def visit(accum, item):
        blocks, source, target, live_count, device = item
        row_index = (device // N_COL).astype(jnp.int32)
        col_index = (device % N_COL).astype(jnp.int32)
        if forward:
            in_start, out_start = col_index * CB, row_index * RB
        else:
            in_start, out_start = row_index * RB, col_index * CB
        local_in = lax.dynamic_slice_in_dim(tiles, in_start, in_count, 0)
        picked = jnp.take(local_in, source, axis=0).astype(jnp.float32)
        products = jnp.einsum(form, blocks.astype(jnp.float32), picked, precision=lax.Precision.HIGHEST)
        live_mask = (slot_index < live_count).astype(jnp.float32)
        selector = (target[:, None] == jnp.arange(out_count, dtype=jnp.int32)[None, :]).astype(jnp.float32) * live_mask[:, None]
        added = jnp.einsum("bo,bik->oik", selector, products, precision=lax.Precision.HIGHEST)
        current = lax.dynamic_slice_in_dim(accum, out_start, out_count, 0)
        accum = lax.dynamic_update_slice_in_dim(accum, current + added, out_start, 0)
        return accum, None

    zero_acc = jnp.zeros((total_out, BS, RANK), jnp.float32)
    return lax.scan(visit, zero_acc, (all_blocks, source_ids, target_ids, all_counts, device_ids))[0]


def reference(block_values, block_rows, block_cols, block_count, basis):
    device_total = N_ROW * N_COL
    all_blocks = block_values.reshape(device_total, BMAX, BS, BS)
    all_rows = block_rows.reshape(device_total, BMAX)
    all_cols = block_cols.reshape(device_total, BMAX)
    all_counts = block_count.reshape(device_total)
    basis_tiles = basis.reshape(N_COL * CB, BS, RANK)
    row_sums = sweep(basis_tiles, N_ROW * RB, all_blocks, all_cols, all_rows, all_counts, True)
    row_basis = row_sums.astype(jnp.bfloat16)
    column_sums = sweep(row_basis, N_COL * CB, all_blocks, all_rows, all_cols, all_counts, False)
    return column_sums.reshape(N_COL * CB * BS, RANK)
```

```python
import functools
import math

import jax
import jax.numpy as jnp
from jax import lax
from jax.experimental import pallas as pl
from jax.experimental.pallas import tpu as pltpu
from jax.sharding import PartitionSpec as P

RB = 8
CB = 8
LANES = 128
EXTRA = 16
MESH = pl.DeviceIdType.MESH


def encode(dst, value):
    rows = value.shape[0]
    top = jnp.max(jnp.abs(value), axis=0, keepdims=True)
    power = jnp.floor(jnp.log2(jnp.maximum(top, 1e-30)))
    scaled = jnp.round(value * jnp.exp2(13.9 - power)).astype(jnp.int32)
    dst[pl.ds(0, rows), :] = scaled.astype(jnp.int16)
    tail = jnp.broadcast_to(power.astype(jnp.int32), (EXTRA, value.shape[1]))
    dst[pl.ds(rows, EXTRA), :] = tail.astype(jnp.int16)


def decode(src):
    rows = src.shape[0] - EXTRA
    power = src[pl.ds(rows, EXTRA), :].astype(jnp.int32).astype(jnp.float32)[0:1, :]
    values = src[pl.ds(0, rows), :].astype(jnp.int32).astype(jnp.float32)
    return values * jnp.exp2(power - 13.9)


def kernel(
    NR, NX, NZ,
    table, basis, blocks, out,
    held, turned, matrix, flipped, gathered, part, xs, xr, zs, zr, row_basis, cs, cr, ys, yr,
    load_sem, g_ss, g_sr, x_ss, x_sr, z_ss, z_sr, az_ss, ax_ss, a_sr, c_ss, c_sr, y_ss, y_sr,
):
    NY = NR // 2
    slots, size, _ = blocks.shape
    chunks = gathered.shape[0]
    share = basis.shape[0]
    piece = part.shape[1] // (NX * NZ)
    depth = gathered.shape[1]
    row = lax.axis_index("row")
    col = lax.axis_index("col")
    y, k = row // 2, row % 2
    z, x = col // NX, col % NX
    other = 1 - k

    def dev(y_, k_, z_, x_):
        return (y_ * 2 + k_, z_ * NX + x_)

    def remote(src, dst, send, recv, to):
        return pltpu.make_async_remote_copy(
            src_ref=src, dst_ref=dst, send_sem=send, recv_sem=recv, device_id=to, device_id_type=MESH
        )

    sends = []

    def start(copy, cond=None):
        sends.append((copy, cond))
        if cond is None:
            copy.start()
        else:
            pl.when(cond)(copy.start)

    load = pltpu.make_async_copy(blocks, held.at[pl.ds(0, slots)], load_sem)
    load.start()

    barrier = pltpu.get_barrier_semaphore()

    def greet(to):
        pl.semaphore_signal(barrier, inc=1, device_id=to, device_id_type=MESH)

    greet(dev(y, other, z, x))
    for dy in range(1, NY):
        greet(dev((y + dy) % NY, k, z, x))
    for dx in range(1, NX):
        greet(dev(y, k, z, (x + dx) % NX))
    pl.when(z > 0)(lambda: greet(dev(y, k, z - 1, x)))
    pl.when(z < NZ - 1)(lambda: greet(dev(y, k, z + 1, x)))
    ends = (z + NZ - 1) // NZ + (2 * NZ - 2 - z) // NZ
    pl.semaphore_wait(barrier, NY + NX - 1 + ends)

    def g_rows(r):
        return pl.ds(pl.multiple_of(r * share, share), share)

    def g_dst(h, r):
        return gathered.at[h, g_rows(r)]

    for h in range(chunks):
        src = basis.at[:, pl.ds(h * LANES, LANES)]
        for dy in range(1, NY):
            start(remote(src, g_dst(h, row), g_ss.at[h, dy], g_sr.at[h, row], dev((y + dy) % NY, k, z, x)))
        start(remote(src, g_dst(h, row), g_ss.at[h, 0], g_sr.at[h, row], dev(y, other, z, x)))
        gathered[h, g_rows(row), :] = basis[:, pl.ds(h * LANES, LANES)]

    def await_recv(dst, sem):
        remote(dst, dst, sem, sem, dev(y, other, z, x)).wait_recv()

    def gather(h):
        for dy in range(1, NY):
            r = ((y + dy) % NY) * 2 + k
            await_recv(g_dst(h, r), g_sr.at[h, r])
            start(remote(g_dst(h, r), g_dst(h, r), g_ss.at[h, NY + dy], g_sr.at[h, r], dev(y, other, z, x)))
        for dy in range(NY):
            r = ((y + dy) % NY) * 2 + other
            await_recv(g_dst(h, r), g_sr.at[h, r])

    held[slots] = jnp.zeros((size, size), held.dtype)
    load.wait()

    def lay(i, _):
        for j in range(CB):
            matrix[pl.ds(pl.multiple_of(i * size, size), size), pl.ds(j * size, size)] = held[table[i * CB + j]]
        return 0

    lax.fori_loop(0, RB, lay, 0)

    def turn_all():
        def turn(s, _):
            turned[s] = held[s].T
            return 0

        lax.fori_loop(0, slots + 1, turn, 0)

        def lay_turned(j, _):
            for i in range(RB):
                flipped[pl.ds(pl.multiple_of(j * size, size), size), pl.ds(i * size, size)] = turned[table[i * CB + j]]
            return 0

        lax.fori_loop(0, CB, lay_turned, 0)

    def p_rows(x_, z_):
        return pl.ds(pl.multiple_of((x_ * NZ + z_) * piece, piece), piece)

    def target(e):
        half = (2 * z) // NZ
        sign = 1 - 2 * half
        near = half * (NZ - 1 - z) + (1 - half) * z
        far = (e - 2 * near - 1 + 2 * NZ) // (2 * NZ)
        away = far * (e - near) + (1 - far) * ((e + 1) // 2)
        way = sign * (far + (1 - far) * (1 - 2 * (e % 2)))
        return z + way * away, way

    def product(h, x_, t):
        rows = p_rows(x_, t)
        return jnp.dot(matrix[rows, :], gathered[h], preferred_element_type=jnp.float32)

    def reduce_x(h):
        for dx in range(1, NX):
            x_ = (x + dx) % NX
            for e in range(NZ - 1, -1, -1):
                t, _ = target(e)
                encode(xs.at[h, dx, t], product(h, x_, t))
                start(remote(xs.at[h, dx, t], xr.at[h, dx, t], x_ss.at[h, dx, t], x_sr.at[h, dx, t], dev(y, k, z, x_)))

        def own(t, _):
            part[h, p_rows(x, t), :] = product(h, x, t)
            return 0

        lax.fori_loop(0, NZ, own, 0)

    def reduce_z(h, e):
        t, way = target(e)
        rows = p_rows(x, t)
        total = part[h, rows, :]
        for dx in range(1, NX):
            await_recv(xr.at[h, dx, t], x_sr.at[h, dx, t])
            total = total + decode(xr.at[h, dx, t])

        def add(flow):
            await_recv(zr.at[h, flow, t], z_sr.at[h, flow, t])
            part[h, rows, :] += decode(zr.at[h, flow, t])

        part[h, rows, :] = total
        if e > 0:
            flow = (1 - way) // 2
            back = z - way
            pl.when((back >= 0) & (back < NZ))(lambda: add(flow))
            encode(zs.at[h, t], part[h, rows, :])
            start(remote(zs.at[h, t], zr.at[h, flow, t], z_ss.at[h, t], z_sr.at[h, flow, t], dev(y, k, z + way, x)))
        else:
            pl.when(z > 0)(lambda: add(0))
            pl.when(z < NZ - 1)(lambda: add(1))
            row_basis[h, rows, :] = part[h, rows, :].astype(row_basis.dtype)

    def spread(h, e):
        t, way = target(e)
        q = x * NZ + t
        ref = row_basis.at[h, p_rows(x, t)]
        if e == 0:
            start(remote(ref, ref, az_ss.at[h, 0, t], a_sr.at[h, q], dev(y, k, z + 1, x)), z < NZ - 1)
            start(remote(ref, ref, az_ss.at[h, 1, t], a_sr.at[h, q], dev(y, k, z - 1, x)), z > 0)
        else:
            await_recv(ref, a_sr.at[h, q])
            onward = z - way
            start(
                remote(ref, ref, az_ss.at[h, 0, t], a_sr.at[h, q], dev(y, k, onward, x)),
                (onward >= 0) & (onward < NZ),
            )
        for dx in range(1, NX):
            start(remote(ref, ref, ax_ss.at[h, dx, t], a_sr.at[h, q], dev(y, k, z, (x + dx) % NX)))

    def collect(h):
        for dx in range(1, NX):
            x_ = (x + dx) % NX
            for t in range(NZ):
                await_recv(row_basis.at[h, p_rows(x_, t)], a_sr.at[h, x_ * NZ + t])

    def back_product(h, r):
        rows = g_rows(r)
        return jnp.dot(flipped[rows, :], row_basis[h], preferred_element_type=jnp.float32)

    def back_core(h):
        for dy in list(range(1, NY)) + [0]:
            y_ = (y + dy) % NY
            cs[h, dy] = back_product(h, y_ * 2 + other).astype(cs.dtype)
            start(remote(cs.at[h, dy], cr.at[h, dy], c_ss.at[h, dy], c_sr.at[h, dy], dev(y, other, z, x)))

    def back_y(h):
        for dy in list(range(1, NY)) + [0]:
            y_ = (y + dy) % NY
            total = back_product(h, y_ * 2 + k)
            await_recv(cr.at[h, dy], c_sr.at[h, dy])
            total = total + cr[h, dy].astype(jnp.float32)
            if dy > 0:
                ys[h, dy] = total.astype(ys.dtype)
                start(remote(ys.at[h, dy], yr.at[h, dy], y_ss.at[h, dy], y_sr.at[h, dy], dev(y_, k, z, x)))
            else:
                out[:, pl.ds(h * LANES, LANES)] = total

    def finish(h):
        total = out[:, pl.ds(h * LANES, LANES)]
        for dy in range(1, NY):
            await_recv(yr.at[h, dy], y_sr.at[h, dy])
            total = total + yr[h, dy].astype(jnp.float32)
        out[:, pl.ds(h * LANES, LANES)] = total

    gather(0)
    reduce_x(0)
    for h in range(1, chunks):
        gather(h)
        reduce_x(h)
    turn_all()
    for e in range(NZ - 1, -1, -1):
        reduce_z(0, e)
    for h in range(chunks):
        for e in range(NZ):
            spread(h, e)
            if h + 1 < chunks:
                reduce_z(h + 1, NZ - 1 - e)
    for h in range(chunks):
        collect(h)
        back_core(h)
        back_y(h)
    for h in range(chunks):
        finish(h)
    for copy, cond in sends:
        if cond is None:
            copy.wait_send()
        else:
            pl.when(cond)(copy.wait_send)


def body(NR, NC, block_values, block_rows, block_cols, block_count, basis):
    blocks = block_values[0, 0]
    slots, size, _ = blocks.shape
    share, rank = basis.shape
    NX = math.isqrt(max(NC // 2, 1))
    if NC % NX:
        NX = 1
    NZ = NC // NX
    NY = NR // 2
    chunks = rank // LANES
    piece = RB * size // NC
    places = jnp.where(
        jnp.arange(slots, dtype=jnp.int32) < block_count[0, 0], block_rows[0, 0] * CB + block_cols[0, 0], -1
    )
    hit = places[None, :] == jnp.arange(RB * CB, dtype=jnp.int32)[:, None]
    table = jnp.min(jnp.where(hit, jnp.arange(slots, dtype=jnp.int32)[None, :], slots), axis=1)
    bf16, i16 = jnp.bfloat16, jnp.int16
    DMA = pltpu.SemaphoreType.DMA
    V = pltpu.VMEM
    return pl.pallas_call(
        functools.partial(kernel, NR, NX, NZ),
        out_shape=jax.ShapeDtypeStruct((share, rank), jnp.float32),
        in_specs=[
            pl.BlockSpec(memory_space=pltpu.SMEM),
            pl.BlockSpec(memory_space=pltpu.VMEM),
            pl.BlockSpec(memory_space=pl.ANY),
        ],
        out_specs=pl.BlockSpec(memory_space=pltpu.VMEM),
        scratch_shapes=[
            V((slots + 1, size, size), bf16),
            V((slots + 1, size, size), bf16),
            V((RB * size, CB * size), bf16),
            V((CB * size, RB * size), bf16),
            V((chunks, CB * size, LANES), bf16),
            V((chunks, RB * size, LANES), jnp.float32),
            V((chunks, NX, NZ, piece + EXTRA, LANES), i16),
            V((chunks, NX, NZ, piece + EXTRA, LANES), i16),
            V((chunks, NZ, piece + EXTRA, LANES), i16),
            V((chunks, 2, NZ, piece + EXTRA, LANES), i16),
            V((chunks, RB * size, LANES), bf16),
            V((chunks, NY, share, LANES), bf16),
            V((chunks, NY, share, LANES), bf16),
            V((chunks, NY, share, LANES), bf16),
            V((chunks, NY, share, LANES), bf16),
            DMA,
            DMA((chunks, 2 * NY)),
            DMA((chunks, NR)),
            DMA((chunks, NX, NZ)),
            DMA((chunks, NX, NZ)),
            DMA((chunks, NZ)),
            DMA((chunks, 2, NZ)),
            DMA((chunks, 2, NZ)),
            DMA((chunks, NX, NZ)),
            DMA((chunks, NC)),
            DMA((chunks, NY)),
            DMA((chunks, NY)),
            DMA((chunks, NY)),
            DMA((chunks, NY)),
        ],
        compiler_params=pltpu.CompilerParams(
            collective_id=0, has_side_effects=True, vmem_limit_bytes=56 * 1024 * 1024
        ),
    )(table, basis, blocks)


def solution(mesh):
    in_specs = (
        P("row", "col", None, None, None),
        P("row", "col", None),
        P("row", "col", None),
        P("row", "col"),
        P(("col", "row"), None),
    )
    out_specs = P(("col", "row"), None)
    run = functools.partial(body, mesh.shape["row"], mesh.shape["col"])
    return jax.shard_map(run, mesh=mesh, in_specs=in_specs, out_specs=out_specs, check_vma=False)
```

```python
import functools
import math

import jax
import jax.numpy as jnp
from jax import lax
from jax.experimental import pallas as pl
from jax.experimental.pallas import tpu as pltpu
from jax.sharding import PartitionSpec as P

RB = 8
CB = 8
LANES = 128
EXTRA = 16
MESH = pl.DeviceIdType.MESH


def encode(dst, value):
    rows = value.shape[0]
    top = jnp.max(jnp.abs(value), axis=0, keepdims=True)
    power = jnp.floor(jnp.log2(jnp.maximum(top, 1e-30)))
    scaled = jnp.round(value * jnp.exp2(13.9 - power)).astype(jnp.int32)
    dst[pl.ds(0, rows), :] = scaled.astype(jnp.int16)
    tail = jnp.broadcast_to(power.astype(jnp.int32), (EXTRA, value.shape[1]))
    dst[pl.ds(rows, EXTRA), :] = tail.astype(jnp.int16)


def decode(src):
    rows = src.shape[0] - EXTRA
    power = src[pl.ds(rows, EXTRA), :].astype(jnp.int32).astype(jnp.float32)[0:1, :]
    values = src[pl.ds(0, rows), :].astype(jnp.int32).astype(jnp.float32)
    return values * jnp.exp2(power - 13.9)


def kernel(
    NR, NX, NZ,
    table, basis, blocks, out,
    held, turned, matrix, flipped, gathered, part, xs, xr, zs, zr, row_basis, cs, cr, ys, yr,
    load_sem, g_ss, g_sr, x_ss, x_sr, z_ss, z_sr, az_ss, ax_ss, a_sr, c_ss, c_sr, y_ss, y_sr,
):
    NY = NR // 2
    slots, size, _ = blocks.shape
    chunks = gathered.shape[0]
    share = basis.shape[0]
    piece = part.shape[1] // (NX * NZ)
    depth = gathered.shape[1]
    row = lax.axis_index("row")
    col = lax.axis_index("col")
    y, k = row // 2, row % 2
    z, x = col // NX, col % NX
    other = 1 - k

    def dev(y_, k_, z_, x_):
        return (y_ * 2 + k_, z_ * NX + x_)

    def remote(src, dst, send, recv, to):
        return pltpu.make_async_remote_copy(
            src_ref=src, dst_ref=dst, send_sem=send, recv_sem=recv, device_id=to, device_id_type=MESH
        )

    sends = []

    def start(copy):
        sends.append(copy)
        copy.start()

    load = pltpu.make_async_copy(blocks, held.at[pl.ds(0, slots)], load_sem)
    load.start()

    barrier = pltpu.get_barrier_semaphore()

    def greet(to):
        pl.semaphore_signal(barrier, inc=1, device_id=to, device_id_type=MESH)

    greet(dev(y, other, z, x))
    for dy in range(1, NY):
        greet(dev((y + dy) % NY, k, z, x))
    for dx in range(1, NX):
        greet(dev(y, k, z, (x + dx) % NX))
    for dz in range(1, NZ):
        greet(dev(y, k, (z + dz) % NZ, x))
    pl.semaphore_wait(barrier, NY + NX + NZ - 2)

    def g_rows(r):
        return pl.ds(pl.multiple_of(r * share, share), share)

    def g_dst(h, r):
        return gathered.at[h, g_rows(r)]

    for h in range(chunks):
        src = basis.at[:, pl.ds(h * LANES, LANES)]
        for dy in range(1, NY):
            start(remote(src, g_dst(h, row), g_ss.at[h, dy], g_sr.at[h, row], dev((y + dy) % NY, k, z, x)))
        start(remote(src, g_dst(h, row), g_ss.at[h, 0], g_sr.at[h, row], dev(y, other, z, x)))
        gathered[h, g_rows(row), :] = basis[:, pl.ds(h * LANES, LANES)]

    def await_recv(dst, sem):
        remote(dst, dst, sem, sem, dev(y, other, z, x)).wait_recv()

    def gather(h):
        for dy in range(1, NY):
            r = ((y + dy) % NY) * 2 + k
            await_recv(g_dst(h, r), g_sr.at[h, r])
            start(remote(g_dst(h, r), g_dst(h, r), g_ss.at[h, NY + dy], g_sr.at[h, r], dev(y, other, z, x)))
        for dy in range(NY):
            r = ((y + dy) % NY) * 2 + other
            await_recv(g_dst(h, r), g_sr.at[h, r])

    held[slots] = jnp.zeros((size, size), held.dtype)
    load.wait()

    def lay(i, _):
        for j in range(CB):
            matrix[pl.ds(pl.multiple_of(i * size, size), size), pl.ds(j * size, size)] = held[table[i * CB + j]]
        return 0

    lax.fori_loop(0, RB, lay, 0)

    def turn_all():
        def turn(s, _):
            turned[s] = held[s].T
            return 0

        lax.fori_loop(0, slots + 1, turn, 0)

        def lay_turned(j, _):
            for i in range(RB):
                flipped[pl.ds(pl.multiple_of(j * size, size), size), pl.ds(i * size, size)] = turned[table[i * CB + j]]
            return 0

        lax.fori_loop(0, CB, lay_turned, 0)

    def p_rows(x_, z_):
        return pl.ds(pl.multiple_of((x_ * NZ + z_) * piece, piece), piece)

    def x_rows(x_):
        return pl.ds(pl.multiple_of(x_ * NZ * piece, NZ * piece), NZ * piece)

    def product(h, x_):
        part[h, x_rows(x_), :] = jnp.dot(matrix[x_rows(x_), :], gathered[h], preferred_element_type=jnp.float32)

    z_order = [(z + dz) % NZ for dz in range(1, NZ)]

    def reduce_x(h):
        for dx in range(1, NX):
            x_ = (x + dx) % NX
            product(h, x_)
            for t in z_order + [z]:
                encode(xs.at[h, dx, t], part[h, p_rows(x_, t), :])
                start(remote(xs.at[h, dx, t], xr.at[h, dx, t], x_ss.at[h, dx, t], x_sr.at[h, dx, t], dev(y, k, z, x_)))
        product(h, x)

    def add_x(h, t):
        total = part[h, p_rows(x, t), :]
        for dx in range(1, NX):
            await_recv(xr.at[h, dx, t], x_sr.at[h, dx, t])
            total = total + decode(xr.at[h, dx, t])
        return total

    def reduce_z(h):
        for dz, t in enumerate(z_order, 1):
            encode(zs.at[h, dz], add_x(h, t))
            start(remote(zs.at[h, dz], zr.at[h, dz], z_ss.at[h, dz], z_sr.at[h, dz], dev(y, k, t, x)))

    def pass_x(h, t):
        ref = row_basis.at[h, p_rows(x, t)]
        for dx in range(1, NX):
            start(remote(ref, ref, ax_ss.at[h, dx, t], a_sr.at[h, x * NZ + t], dev(y, k, z, (x + dx) % NX)))

    def settle(h):
        total = add_x(h, z)
        for dz in range(1, NZ):
            await_recv(zr.at[h, dz], z_sr.at[h, dz])
            total = total + decode(zr.at[h, dz])
        row_basis[h, p_rows(x, z), :] = total.astype(row_basis.dtype)
        ref = row_basis.at[h, p_rows(x, z)]
        for dz, t in enumerate(z_order, 1):
            start(remote(ref, ref, az_ss.at[h, dz], a_sr.at[h, x * NZ + z], dev(y, k, t, x)))
        pass_x(h, z)

    def spread(h):
        for t in z_order:
            await_recv(row_basis.at[h, p_rows(x, t)], a_sr.at[h, x * NZ + t])
            pass_x(h, t)

    def back_half(h, x_):
        return jnp.dot(flipped[:, x_rows(x_)], row_basis[h, x_rows(x_), :], preferred_element_type=jnp.float32)

    def back_own(h):
        part[h] = back_half(h, x)

    def collect(h):
        for dx in range(1, NX):
            x_ = (x + dx) % NX
            for t in range(NZ):
                await_recv(row_basis.at[h, p_rows(x_, t)], a_sr.at[h, x_ * NZ + t])

    def back_product(h, r):
        rows = g_rows(r)
        total = part[h, rows, :]
        for dx in range(1, NX):
            x_ = (x + dx) % NX
            total = total + jnp.dot(
                flipped[rows, x_rows(x_)], row_basis[h, x_rows(x_), :], preferred_element_type=jnp.float32
            )
        return total

    def back_core(h):
        for dy in list(range(1, NY)) + [0]:
            y_ = (y + dy) % NY
            cs[h, dy] = back_product(h, y_ * 2 + other).astype(cs.dtype)
            start(remote(cs.at[h, dy], cr.at[h, dy], c_ss.at[h, dy], c_sr.at[h, dy], dev(y, other, z, x)))

    def back_y(h):
        for dy in list(range(1, NY)) + [0]:
            y_ = (y + dy) % NY
            total = back_product(h, y_ * 2 + k)
            await_recv(cr.at[h, dy], c_sr.at[h, dy])
            total = total + cr[h, dy].astype(jnp.float32)
            if dy > 0:
                ys[h, dy] = total.astype(ys.dtype)
                start(remote(ys.at[h, dy], yr.at[h, dy], y_ss.at[h, dy], y_sr.at[h, dy], dev(y_, k, z, x)))
            else:
                out[:, pl.ds(h * LANES, LANES)] = total

    def finish(h):
        total = out[:, pl.ds(h * LANES, LANES)]
        for dy in range(1, NY):
            await_recv(yr.at[h, dy], y_sr.at[h, dy])
            total = total + yr[h, dy].astype(jnp.float32)
        out[:, pl.ds(h * LANES, LANES)] = total

    gather(0)
    reduce_x(0)
    for h in range(1, chunks):
        gather(h)
        reduce_x(h)
    turn_all()
    for h in range(chunks):
        reduce_z(h)
        if h > 0:
            spread(h - 1)
        settle(h)
        if h > 0:
            back_own(h - 1)
    spread(chunks - 1)
    for h in range(chunks):
        collect(h)
        back_core(h)
        back_y(h)
        if h + 1 == chunks - 1:
            back_own(h + 1)
    for h in range(chunks):
        finish(h)
    for copy in sends:
        copy.wait_send()


def body(NR, NC, block_values, block_rows, block_cols, block_count, basis):
    blocks = block_values[0, 0]
    slots, size, _ = blocks.shape
    share, rank = basis.shape
    NX = math.isqrt(max(NC // 2, 1))
    if NC % NX:
        NX = 1
    NZ = NC // NX
    NY = NR // 2
    chunks = rank // LANES
    piece = RB * size // NC
    places = jnp.where(
        jnp.arange(slots, dtype=jnp.int32) < block_count[0, 0], block_rows[0, 0] * CB + block_cols[0, 0], -1
    )
    hit = places[None, :] == jnp.arange(RB * CB, dtype=jnp.int32)[:, None]
    table = jnp.min(jnp.where(hit, jnp.arange(slots, dtype=jnp.int32)[None, :], slots), axis=1)
    bf16, i16 = jnp.bfloat16, jnp.int16
    DMA = pltpu.SemaphoreType.DMA
    V = pltpu.VMEM
    return pl.pallas_call(
        functools.partial(kernel, NR, NX, NZ),
        out_shape=jax.ShapeDtypeStruct((share, rank), jnp.float32),
        in_specs=[
            pl.BlockSpec(memory_space=pltpu.SMEM),
            pl.BlockSpec(memory_space=pltpu.VMEM),
            pl.BlockSpec(memory_space=pl.ANY),
        ],
        out_specs=pl.BlockSpec(memory_space=pltpu.VMEM),
        scratch_shapes=[
            V((slots + 1, size, size), bf16),
            V((slots + 1, size, size), bf16),
            V((RB * size, CB * size), bf16),
            V((CB * size, RB * size), bf16),
            V((chunks, CB * size, LANES), bf16),
            V((chunks, RB * size, LANES), jnp.float32),
            V((chunks, NX, NZ, piece + EXTRA, LANES), i16),
            V((chunks, NX, NZ, piece + EXTRA, LANES), i16),
            V((chunks, NZ, piece + EXTRA, LANES), i16),
            V((chunks, NZ, piece + EXTRA, LANES), i16),
            V((chunks, RB * size, LANES), bf16),
            V((chunks, NY, share, LANES), bf16),
            V((chunks, NY, share, LANES), bf16),
            V((chunks, NY, share, LANES), bf16),
            V((chunks, NY, share, LANES), bf16),
            DMA,
            DMA((chunks, 2 * NY)),
            DMA((chunks, NR)),
            DMA((chunks, NX, NZ)),
            DMA((chunks, NX, NZ)),
            DMA((chunks, NZ)),
            DMA((chunks, NZ)),
            DMA((chunks, NZ)),
            DMA((chunks, NX, NZ)),
            DMA((chunks, NC)),
            DMA((chunks, NY)),
            DMA((chunks, NY)),
            DMA((chunks, NY)),
            DMA((chunks, NY)),
        ],
        compiler_params=pltpu.CompilerParams(
            collective_id=0, has_side_effects=True, vmem_limit_bytes=56 * 1024 * 1024
        ),
    )(table, basis, blocks)


def solution(mesh):
    in_specs = (
        P("row", "col", None, None, None),
        P("row", "col", None),
        P("row", "col", None),
        P("row", "col"),
        P(("col", "row"), None),
    )
    out_specs = P(("col", "row"), None)
    run = functools.partial(body, mesh.shape["row"], mesh.shape["col"])
    return jax.shard_map(run, mesh=mesh, in_specs=in_specs, out_specs=out_specs, check_vma=False)
```

```python
import functools
import math

import jax
import jax.numpy as jnp
from jax import lax
from jax.experimental import pallas as pl
from jax.experimental.pallas import tpu as pltpu
from jax.sharding import PartitionSpec as P

RB = 8
CB = 8
LANES = 128
EXTRA = 16
MESH = pl.DeviceIdType.MESH


def encode(dst, value):
    rows = value.shape[0]
    top = jnp.max(jnp.abs(value), axis=0, keepdims=True)
    power = jnp.floor(jnp.log2(jnp.maximum(top, 1e-30)))
    scaled = jnp.round(value * jnp.exp2(13.9 - power)).astype(jnp.int32)
    dst[pl.ds(0, rows), :] = scaled.astype(jnp.int16)
    tail = jnp.broadcast_to(power.astype(jnp.int32), (EXTRA, value.shape[1]))
    dst[pl.ds(rows, EXTRA), :] = tail.astype(jnp.int16)


def decode(src):
    rows = src.shape[0] - EXTRA
    power = src[pl.ds(rows, EXTRA), :].astype(jnp.int32).astype(jnp.float32)[0:1, :]
    values = src[pl.ds(0, rows), :].astype(jnp.int32).astype(jnp.float32)
    return values * jnp.exp2(power - 13.9)


def kernel(
    NR, NX, NZ,
    table, basis, blocks, out,
    held, turned, matrix, flipped, gathered, part, xs, xr, zs, zr, row_basis, cs, cr, ys, yr,
    load_sem, g_ss, g_sr, x_ss, x_sr, z_ss, z_sr, az_ss, ax_ss, a_sr, c_ss, c_sr, y_ss, y_sr,
):
    NY = NR // 2
    slots, size, _ = blocks.shape
    chunks = gathered.shape[0]
    share = basis.shape[0]
    piece = part.shape[1] // (NX * NZ)
    depth = gathered.shape[1]
    row = lax.axis_index("row")
    col = lax.axis_index("col")
    y, k = row // 2, row % 2
    z, x = col // NX, col % NX
    other = 1 - k

    def dev(y_, k_, z_, x_):
        return (y_ * 2 + k_, z_ * NX + x_)

    def remote(src, dst, send, recv, to):
        return pltpu.make_async_remote_copy(
            src_ref=src, dst_ref=dst, send_sem=send, recv_sem=recv, device_id=to, device_id_type=MESH
        )

    sends = []

    def start(copy):
        sends.append(copy)
        copy.start()

    load = pltpu.make_async_copy(blocks, held.at[pl.ds(0, slots)], load_sem)
    load.start()

    barrier = pltpu.get_barrier_semaphore()

    def greet(to):
        pl.semaphore_signal(barrier, inc=1, device_id=to, device_id_type=MESH)

    greet(dev(y, other, z, x))
    for dy in range(1, NY):
        greet(dev((y + dy) % NY, k, z, x))
    for dx in range(1, NX):
        greet(dev(y, k, z, (x + dx) % NX))
    for dz in range(1, NZ):
        greet(dev(y, k, (z + dz) % NZ, x))
    pl.semaphore_wait(barrier, NY + NX + NZ - 2)

    def g_rows(r):
        return pl.ds(pl.multiple_of(r * share, share), share)

    def g_dst(h, r):
        return gathered.at[h, g_rows(r)]

    for h in range(chunks):
        src = basis.at[:, pl.ds(h * LANES, LANES)]
        for dy in range(1, NY):
            start(remote(src, g_dst(h, row), g_ss.at[h, dy], g_sr.at[h, row], dev((y + dy) % NY, k, z, x)))
        start(remote(src, g_dst(h, row), g_ss.at[h, 0], g_sr.at[h, row], dev(y, other, z, x)))
        gathered[h, g_rows(row), :] = basis[:, pl.ds(h * LANES, LANES)]

    def await_recv(dst, sem):
        remote(dst, dst, sem, sem, dev(y, other, z, x)).wait_recv()

    def gather(h):
        for dy in range(1, NY):
            r = ((y + dy) % NY) * 2 + k
            await_recv(g_dst(h, r), g_sr.at[h, r])
            start(remote(g_dst(h, r), g_dst(h, r), g_ss.at[h, NY + dy], g_sr.at[h, r], dev(y, other, z, x)))
        for dy in range(NY):
            r = ((y + dy) % NY) * 2 + other
            await_recv(g_dst(h, r), g_sr.at[h, r])

    held[slots] = jnp.zeros((size, size), held.dtype)
    load.wait()

    def lay(i, _):
        for j in range(CB):
            matrix[pl.ds(pl.multiple_of(i * size, size), size), pl.ds(j * size, size)] = held[table[i * CB + j]]
        return 0

    lax.fori_loop(0, RB, lay, 0)

    def turn_all():
        def turn(s, _):
            turned[s] = held[s].T
            return 0

        lax.fori_loop(0, slots + 1, turn, 0)

        def lay_turned(j, _):
            for i in range(RB):
                flipped[pl.ds(pl.multiple_of(j * size, size), size), pl.ds(i * size, size)] = turned[table[i * CB + j]]
            return 0

        lax.fori_loop(0, CB, lay_turned, 0)

    def p_rows(x_, z_):
        return pl.ds(pl.multiple_of((x_ * NZ + z_) * piece, piece), piece)

    def x_rows(x_):
        return pl.ds(pl.multiple_of(x_ * NZ * piece, NZ * piece), NZ * piece)

    def product(h, x_):
        part[h, x_rows(x_), :] = jnp.dot(matrix[x_rows(x_), :], gathered[h], preferred_element_type=jnp.float32)

    z_order = [(z + dz) % NZ for dz in range(1, NZ)]

    def reduce_x(h):
        for dx in range(1, NX):
            x_ = (x + dx) % NX
            product(h, x_)
            for t in z_order + [z]:
                encode(xs.at[h, dx, t], part[h, p_rows(x_, t), :])
                start(remote(xs.at[h, dx, t], xr.at[h, dx, t], x_ss.at[h, dx, t], x_sr.at[h, dx, t], dev(y, k, z, x_)))

    def add_x(h, t):
        total = part[h, p_rows(x, t), :]
        for dx in range(1, NX):
            await_recv(xr.at[h, dx, t], x_sr.at[h, dx, t])
            total = total + decode(xr.at[h, dx, t])
        return total

    def reduce_z(h):
        for dz, t in enumerate(z_order, 1):
            encode(zs.at[h, dz], add_x(h, t))
            start(remote(zs.at[h, dz], zr.at[h, dz], z_ss.at[h, dz], z_sr.at[h, dz], dev(y, k, t, x)))

    def pass_x(h, t):
        ref = row_basis.at[h, p_rows(x, t)]
        for dx in range(1, NX):
            start(remote(ref, ref, ax_ss.at[h, dx, t], a_sr.at[h, x * NZ + t], dev(y, k, z, (x + dx) % NX)))

    def settle(h):
        total = add_x(h, z)
        for dz in range(1, NZ):
            await_recv(zr.at[h, dz], z_sr.at[h, dz])
            total = total + decode(zr.at[h, dz])
        row_basis[h, p_rows(x, z), :] = total.astype(row_basis.dtype)
        ref = row_basis.at[h, p_rows(x, z)]
        for dz, t in enumerate(z_order, 1):
            start(remote(ref, ref, az_ss.at[h, dz], a_sr.at[h, x * NZ + z], dev(y, k, t, x)))
        pass_x(h, z)

    def spread(h):
        for t in z_order:
            await_recv(row_basis.at[h, p_rows(x, t)], a_sr.at[h, x * NZ + t])
            pass_x(h, t)

    def back_half(h, x_):
        return jnp.dot(flipped[:, x_rows(x_)], row_basis[h, x_rows(x_), :], preferred_element_type=jnp.float32)

    def back_own(h):
        part[h] = back_half(h, x)

    def collect(h):
        for dx in range(1, NX):
            x_ = (x + dx) % NX
            for t in range(NZ):
                await_recv(row_basis.at[h, p_rows(x_, t)], a_sr.at[h, x_ * NZ + t])

    def back_product(h, r):
        rows = g_rows(r)
        total = part[h, rows, :]
        for dx in range(1, NX):
            x_ = (x + dx) % NX
            total = total + jnp.dot(
                flipped[rows, x_rows(x_)], row_basis[h, x_rows(x_), :], preferred_element_type=jnp.float32
            )
        return total

    def back_core(h):
        for dy in list(range(1, NY)) + [0]:
            y_ = (y + dy) % NY
            cs[h, dy] = back_product(h, y_ * 2 + other).astype(cs.dtype)
            start(remote(cs.at[h, dy], cr.at[h, dy], c_ss.at[h, dy], c_sr.at[h, dy], dev(y, other, z, x)))

    def back_y(h):
        for dy in list(range(1, NY)) + [0]:
            y_ = (y + dy) % NY
            total = back_product(h, y_ * 2 + k)
            await_recv(cr.at[h, dy], c_sr.at[h, dy])
            total = total + cr[h, dy].astype(jnp.float32)
            if dy > 0:
                ys[h, dy] = total.astype(ys.dtype)
                start(remote(ys.at[h, dy], yr.at[h, dy], y_ss.at[h, dy], y_sr.at[h, dy], dev(y_, k, z, x)))
            else:
                out[:, pl.ds(h * LANES, LANES)] = total

    def finish(h):
        total = out[:, pl.ds(h * LANES, LANES)]
        for dy in range(1, NY):
            await_recv(yr.at[h, dy], y_sr.at[h, dy])
            total = total + yr[h, dy].astype(jnp.float32)
        out[:, pl.ds(h * LANES, LANES)] = total

    turn_all()
    gather(0)
    reduce_x(0)
    product(0, x)
    for h in range(1, chunks):
        gather(h)
        reduce_x(h)
        reduce_z(h - 1)
        product(h, x)
        settle(h - 1)
        if h > 1:
            spread(h - 2)
            back_own(h - 2)
    last = chunks - 1
    reduce_z(last)
    if last > 0:
        spread(last - 1)
    settle(last)
    if last > 0:
        back_own(last - 1)
    spread(last)
    for h in range(chunks):
        if h == last:
            back_own(h)
        collect(h)
        back_core(h)
        back_y(h)
    for h in range(chunks):
        finish(h)
    for copy in sends:
        copy.wait_send()


def body(NR, NC, block_values, block_rows, block_cols, block_count, basis):
    blocks = block_values[0, 0]
    slots, size, _ = blocks.shape
    share, rank = basis.shape
    NX = math.isqrt(max(NC // 2, 1))
    if NC % NX:
        NX = 1
    NZ = NC // NX
    NY = NR // 2
    chunks = rank // LANES
    piece = RB * size // NC
    places = jnp.where(
        jnp.arange(slots, dtype=jnp.int32) < block_count[0, 0], block_rows[0, 0] * CB + block_cols[0, 0], -1
    )
    hit = places[None, :] == jnp.arange(RB * CB, dtype=jnp.int32)[:, None]
    table = jnp.min(jnp.where(hit, jnp.arange(slots, dtype=jnp.int32)[None, :], slots), axis=1)
    bf16, i16 = jnp.bfloat16, jnp.int16
    DMA = pltpu.SemaphoreType.DMA
    V = pltpu.VMEM
    return pl.pallas_call(
        functools.partial(kernel, NR, NX, NZ),
        out_shape=jax.ShapeDtypeStruct((share, rank), jnp.float32),
        in_specs=[
            pl.BlockSpec(memory_space=pltpu.SMEM),
            pl.BlockSpec(memory_space=pltpu.VMEM),
            pl.BlockSpec(memory_space=pl.ANY),
        ],
        out_specs=pl.BlockSpec(memory_space=pltpu.VMEM),
        scratch_shapes=[
            V((slots + 1, size, size), bf16),
            V((slots + 1, size, size), bf16),
            V((RB * size, CB * size), bf16),
            V((CB * size, RB * size), bf16),
            V((chunks, CB * size, LANES), bf16),
            V((chunks, RB * size, LANES), jnp.float32),
            V((chunks, NX, NZ, piece + EXTRA, LANES), i16),
            V((chunks, NX, NZ, piece + EXTRA, LANES), i16),
            V((chunks, NZ, piece + EXTRA, LANES), i16),
            V((chunks, NZ, piece + EXTRA, LANES), i16),
            V((chunks, RB * size, LANES), bf16),
            V((chunks, NY, share, LANES), bf16),
            V((chunks, NY, share, LANES), bf16),
            V((chunks, NY, share, LANES), bf16),
            V((chunks, NY, share, LANES), bf16),
            DMA,
            DMA((chunks, 2 * NY)),
            DMA((chunks, NR)),
            DMA((chunks, NX, NZ)),
            DMA((chunks, NX, NZ)),
            DMA((chunks, NZ)),
            DMA((chunks, NZ)),
            DMA((chunks, NZ)),
            DMA((chunks, NX, NZ)),
            DMA((chunks, NC)),
            DMA((chunks, NY)),
            DMA((chunks, NY)),
            DMA((chunks, NY)),
            DMA((chunks, NY)),
        ],
        compiler_params=pltpu.CompilerParams(
            collective_id=0, has_side_effects=True, vmem_limit_bytes=56 * 1024 * 1024
        ),
    )(table, basis, blocks)


def solution(mesh):
    in_specs = (
        P("row", "col", None, None, None),
        P("row", "col", None),
        P("row", "col", None),
        P("row", "col"),
        P(("col", "row"), None),
    )
    out_specs = P(("col", "row"), None)
    run = functools.partial(body, mesh.shape["row"], mesh.shape["col"])
    return jax.shard_map(run, mesh=mesh, in_specs=in_specs, out_specs=out_specs, check_vma=False)
```

```python
import functools
import math

import jax
import jax.numpy as jnp
from jax import lax
from jax.experimental import pallas as pl
from jax.experimental.pallas import tpu as pltpu
from jax.sharding import PartitionSpec as P

RB = 8
CB = 8
LANES = 128
EXTRA = 16
MESH = pl.DeviceIdType.MESH


def encode(dst, value):
    rows = value.shape[0]
    top = jnp.max(jnp.abs(value), axis=0, keepdims=True)
    power = jnp.floor(jnp.log2(jnp.maximum(top, 1e-30)))
    scaled = jnp.round(value * jnp.exp2(13.9 - power)).astype(jnp.int32)
    dst[pl.ds(0, rows), :] = scaled.astype(jnp.int16)
    tail = jnp.broadcast_to(power.astype(jnp.int32), (EXTRA, value.shape[1]))
    dst[pl.ds(rows, EXTRA), :] = tail.astype(jnp.int16)


def decode(src):
    rows = src.shape[0] - EXTRA
    power = src[pl.ds(rows, EXTRA), :].astype(jnp.int32).astype(jnp.float32)[0:1, :]
    values = src[pl.ds(0, rows), :].astype(jnp.int32).astype(jnp.float32)
    return values * jnp.exp2(power - 13.9)


def kernel(
    NR, NX, NZ,
    table, basis, blocks, out,
    held, turned, matrix, flipped, gathered, part, xs, xr, zs, zr, row_basis, cs, cr, ys, yr,
    load_sem, g_ss, g_sr, x_ss, x_sr, z_ss, z_sr, az_ss, ax_ss, a_sr, c_ss, c_sr, y_ss, y_sr,
):
    NY = NR // 2
    slots, size, _ = blocks.shape
    chunks = part.shape[0]
    share = basis.shape[0]
    piece = part.shape[1] // (NX * NZ)
    row = lax.axis_index("row")
    col = lax.axis_index("col")
    y, k = row // 2, row % 2
    z, x = col // NX, col % NX
    other = 1 - k

    def dev(y_, k_, z_, x_):
        return (y_ * 2 + k_, z_ * NX + x_)

    def remote(src, dst, send, recv, to):
        return pltpu.make_async_remote_copy(
            src_ref=src, dst_ref=dst, send_sem=send, recv_sem=recv, device_id=to, device_id_type=MESH
        )

    sends = []

    def start(copy):
        sends.append(copy)
        copy.start()

    load = pltpu.make_async_copy(blocks, held.at[pl.ds(0, slots)], load_sem)
    load.start()

    barrier = pltpu.get_barrier_semaphore()

    def greet(to):
        pl.semaphore_signal(barrier, inc=1, device_id=to, device_id_type=MESH)

    greet(dev(y, other, z, x))
    for dy in range(1, NY):
        greet(dev((y + dy) % NY, k, z, x))
    for dx in range(1, NX):
        greet(dev(y, k, z, (x + dx) % NX))
    for dz in range(1, NZ):
        greet(dev(y, k, (z + dz) % NZ, x))
    pl.semaphore_wait(barrier, NY + NX + NZ - 2)

    def g_rows(r):
        return pl.ds(pl.multiple_of(r * share, share), share)

    def g_dst(h, r):
        return gathered.at[g_rows(r), pl.ds(h * LANES, LANES)]

    for h in range(chunks):
        src = basis.at[:, pl.ds(h * LANES, LANES)]
        for dy in range(1, NY):
            start(remote(src, g_dst(h, row), g_ss.at[h, dy], g_sr.at[h, row], dev((y + dy) % NY, k, z, x)))
        start(remote(src, g_dst(h, row), g_ss.at[h, 0], g_sr.at[h, row], dev(y, other, z, x)))

    gathered[g_rows(row), :] = basis[...]

    def await_recv(dst, sem):
        remote(dst, dst, sem, sem, dev(y, other, z, x)).wait_recv()

    def gather(h):
        for dy in range(1, NY):
            r = ((y + dy) % NY) * 2 + k
            await_recv(g_dst(h, r), g_sr.at[h, r])
            start(remote(g_dst(h, r), g_dst(h, r), g_ss.at[h, NY + dy], g_sr.at[h, r], dev(y, other, z, x)))

    def gather_rest(h):
        for dy in range(NY):
            r = ((y + dy) % NY) * 2 + other
            await_recv(g_dst(h, r), g_sr.at[h, r])

    held[slots] = jnp.zeros((size, size), held.dtype)
    load.wait()

    def lay(i, _):
        for j in range(CB):
            matrix[pl.ds(pl.multiple_of(i * size, size), size), pl.ds(j * size, size)] = held[table[i * CB + j]]
        return 0

    lax.fori_loop(0, RB, lay, 0)

    def turn_all():
        def turn(s, _):
            turned[s] = held[s].T
            return 0

        lax.fori_loop(0, slots + 1, turn, 0)

    def lay_all():
        def lay_turned(j, _):
            for i in range(RB):
                flipped[pl.ds(pl.multiple_of(j * size, size), size), pl.ds(i * size, size)] = turned[table[i * CB + j]]
            return 0

        lax.fori_loop(0, CB, lay_turned, 0)

    def p_rows(x_, z_):
        return pl.ds(pl.multiple_of((x_ * NZ + z_) * piece, piece), piece)

    def x_rows(x_):
        return pl.ds(pl.multiple_of(x_ * NZ * piece, NZ * piece), NZ * piece)

    def product(x_):
        rows = x_rows(x_)
        result = jnp.dot(matrix[rows, :], gathered[...], preferred_element_type=jnp.float32)
        for h in range(chunks):
            part[h, rows, :] = result[:, h * LANES : (h + 1) * LANES]

    z_order = [(z + dz) % NZ for dz in range(1, NZ)]

    def reduce_x(h):
        for dx in range(1, NX):
            x_ = (x + dx) % NX
            for t in z_order + [z]:
                encode(xs.at[h, dx, t], part[h, p_rows(x_, t), :])
                start(remote(xs.at[h, dx, t], xr.at[h, dx, t], x_ss.at[h, dx, t], x_sr.at[h, dx, t], dev(y, k, z, x_)))

    def add_x(h, t):
        total = part[h, p_rows(x, t), :]
        for dx in range(1, NX):
            await_recv(xr.at[h, dx, t], x_sr.at[h, dx, t])
            total = total + decode(xr.at[h, dx, t])
        return total

    def reduce_z(h):
        for dz, t in enumerate(z_order, 1):
            encode(zs.at[h, dz], add_x(h, t))
            start(remote(zs.at[h, dz], zr.at[h, dz], z_ss.at[h, dz], z_sr.at[h, dz], dev(y, k, t, x)))

    def pass_x(h, t):
        ref = row_basis.at[h, p_rows(x, t)]
        for dx in range(1, NX):
            start(remote(ref, ref, ax_ss.at[h, dx, t], a_sr.at[h, x * NZ + t], dev(y, k, z, (x + dx) % NX)))

    def settle(h):
        total = add_x(h, z)
        for dz in range(1, NZ):
            await_recv(zr.at[h, dz], z_sr.at[h, dz])
            total = total + decode(zr.at[h, dz])
        row_basis[h, p_rows(x, z), :] = total.astype(row_basis.dtype)
        ref = row_basis.at[h, p_rows(x, z)]
        for dz, t in enumerate(z_order, 1):
            start(remote(ref, ref, az_ss.at[h, dz], a_sr.at[h, x * NZ + z], dev(y, k, t, x)))
        pass_x(h, z)

    def spread(h):
        for t in z_order:
            await_recv(row_basis.at[h, p_rows(x, t)], a_sr.at[h, x * NZ + t])
            pass_x(h, t)

    def back_half(h, x_):
        return jnp.dot(flipped[:, x_rows(x_)], row_basis[h, x_rows(x_), :], preferred_element_type=jnp.float32)

    def back_own(h):
        part[h] = back_half(h, x)

    def collect(h):
        for dx in range(1, NX):
            x_ = (x + dx) % NX
            for t in range(NZ):
                await_recv(row_basis.at[h, p_rows(x_, t)], a_sr.at[h, x_ * NZ + t])

    def back_product(h, r):
        rows = g_rows(r)
        total = part[h, rows, :]
        for dx in range(1, NX):
            x_ = (x + dx) % NX
            total = total + jnp.dot(
                flipped[rows, x_rows(x_)], row_basis[h, x_rows(x_), :], preferred_element_type=jnp.float32
            )
        return total

    def back_core(h):
        for dy in list(range(1, NY)) + [0]:
            y_ = (y + dy) % NY
            cs[h, dy] = back_product(h, y_ * 2 + other).astype(cs.dtype)
            start(remote(cs.at[h, dy], cr.at[h, dy], c_ss.at[h, dy], c_sr.at[h, dy], dev(y, other, z, x)))

    def back_y(h):
        for dy in list(range(1, NY)) + [0]:
            y_ = (y + dy) % NY
            total = back_product(h, y_ * 2 + k)
            await_recv(cr.at[h, dy], c_sr.at[h, dy])
            total = total + cr[h, dy].astype(jnp.float32)
            if dy > 0:
                ys[h, dy] = total.astype(ys.dtype)
                start(remote(ys.at[h, dy], yr.at[h, dy], y_ss.at[h, dy], y_sr.at[h, dy], dev(y_, k, z, x)))
            else:
                out[:, pl.ds(h * LANES, LANES)] = total

    def finish(h):
        total = out[:, pl.ds(h * LANES, LANES)]
        for dy in range(1, NY):
            await_recv(yr.at[h, dy], y_sr.at[h, dy])
            total = total + yr[h, dy].astype(jnp.float32)
        out[:, pl.ds(h * LANES, LANES)] = total

    turn_all()
    for h in range(chunks):
        gather(h)
    for h in range(chunks):
        gather_rest(h)
    for dx in range(1, NX):
        product((x + dx) % NX)
    for h in range(chunks):
        reduce_x(h)
    product(x)
    for h in range(chunks - 1):
        reduce_z(h)
        if h == 0:
            lay_all()
        settle(h)
        if h > 0:
            spread(h - 1)
            back_own(h - 1)
    if chunks == 1:
        lay_all()
    last = chunks - 1
    reduce_z(last)
    if last > 0:
        spread(last - 1)
    settle(last)
    if last > 0:
        back_own(last - 1)
    spread(last)
    for h in range(chunks):
        if h == last:
            back_own(h)
        collect(h)
        back_core(h)
        back_y(h)
    for h in range(chunks):
        finish(h)
    for copy in sends:
        copy.wait_send()


def body(NR, NC, block_values, block_rows, block_cols, block_count, basis):
    blocks = block_values[0, 0]
    slots, size, _ = blocks.shape
    share, rank = basis.shape
    NX = math.isqrt(max(NC // 2, 1))
    if NC % NX:
        NX = 1
    NZ = NC // NX
    NY = NR // 2
    chunks = rank // LANES
    piece = RB * size // NC
    places = jnp.where(
        jnp.arange(slots, dtype=jnp.int32) < block_count[0, 0], block_rows[0, 0] * CB + block_cols[0, 0], -1
    )
    hit = places[None, :] == jnp.arange(RB * CB, dtype=jnp.int32)[:, None]
    table = jnp.min(jnp.where(hit, jnp.arange(slots, dtype=jnp.int32)[None, :], slots), axis=1)
    bf16, i16 = jnp.bfloat16, jnp.int16
    DMA = pltpu.SemaphoreType.DMA
    V = pltpu.VMEM
    return pl.pallas_call(
        functools.partial(kernel, NR, NX, NZ),
        out_shape=jax.ShapeDtypeStruct((share, rank), jnp.float32),
        in_specs=[
            pl.BlockSpec(memory_space=pltpu.SMEM),
            pl.BlockSpec(memory_space=pltpu.VMEM),
            pl.BlockSpec(memory_space=pl.ANY),
        ],
        out_specs=pl.BlockSpec(memory_space=pltpu.VMEM),
        scratch_shapes=[
            V((slots + 1, size, size), bf16),
            V((slots + 1, size, size), bf16),
            V((RB * size, CB * size), bf16),
            V((CB * size, RB * size), bf16),
            V((CB * size, rank), bf16),
            V((chunks, RB * size, LANES), jnp.float32),
            V((chunks, NX, NZ, piece + EXTRA, LANES), i16),
            V((chunks, NX, NZ, piece + EXTRA, LANES), i16),
            V((chunks, NZ, piece + EXTRA, LANES), i16),
            V((chunks, NZ, piece + EXTRA, LANES), i16),
            V((chunks, RB * size, LANES), bf16),
            V((chunks, NY, share, LANES), bf16),
            V((chunks, NY, share, LANES), bf16),
            V((chunks, NY, share, LANES), bf16),
            V((chunks, NY, share, LANES), bf16),
            DMA,
            DMA((chunks, 2 * NY)),
            DMA((chunks, NR)),
            DMA((chunks, NX, NZ)),
            DMA((chunks, NX, NZ)),
            DMA((chunks, NZ)),
            DMA((chunks, NZ)),
            DMA((chunks, NZ)),
            DMA((chunks, NX, NZ)),
            DMA((chunks, NC)),
            DMA((chunks, NY)),
            DMA((chunks, NY)),
            DMA((chunks, NY)),
            DMA((chunks, NY)),
        ],
        compiler_params=pltpu.CompilerParams(
            collective_id=0, has_side_effects=True, vmem_limit_bytes=56 * 1024 * 1024
        ),
    )(table, basis, blocks)


def solution(mesh):
    in_specs = (
        P("row", "col", None, None, None),
        P("row", "col", None),
        P("row", "col", None),
        P("row", "col"),
        P(("col", "row"), None),
    )
    out_specs = P(("col", "row"), None)
    run = functools.partial(body, mesh.shape["row"], mesh.shape["col"])
    return jax.shard_map(run, mesh=mesh, in_specs=in_specs, out_specs=out_specs, check_vma=False)
```

```python
import functools
import math

import jax
import jax.numpy as jnp
from jax import lax
from jax.experimental import pallas as pl
from jax.experimental.pallas import tpu as pltpu
from jax.sharding import PartitionSpec as P

RB = 8
CB = 8
LANES = 128
EXTRA = 16
MESH = pl.DeviceIdType.MESH


def encode(dst, value):
    rows = value.shape[0]
    top = jnp.max(jnp.abs(value), axis=0, keepdims=True)
    power = jnp.floor(jnp.log2(jnp.maximum(top, 1e-30)))
    scaled = jnp.round(value * jnp.exp2(13.9 - power)).astype(jnp.int32)
    dst[pl.ds(0, rows), :] = scaled.astype(jnp.int16)
    tail = jnp.broadcast_to(power.astype(jnp.int32), (EXTRA, value.shape[1]))
    dst[pl.ds(rows, EXTRA), :] = tail.astype(jnp.int16)


def decode(src):
    rows = src.shape[0] - EXTRA
    power = src[pl.ds(rows, EXTRA), :].astype(jnp.int32).astype(jnp.float32)[0:1, :]
    values = src[pl.ds(0, rows), :].astype(jnp.int32).astype(jnp.float32)
    return values * jnp.exp2(power - 13.9)


def kernel(
    NR, NX, NZ,
    table, basis, blocks, out,
    held, turned, matrix, flipped, gathered, part, xs, xr, zs, zr, row_basis, cs, cr, ys, yr,
    load_sem, g_ss, g_sr, x_ss, x_sr, z_ss, z_sr, az_ss, ax_ss, a_sr, c_ss, c_sr, y_ss, y_sr,
):
    NY = NR // 2
    slots, size, _ = blocks.shape
    chunks = part.shape[0]
    share = basis.shape[0]
    piece = part.shape[1] // (NX * NZ)
    row = lax.axis_index("row")
    col = lax.axis_index("col")
    y, k = row // 2, row % 2
    z, x = col // NX, col % NX
    other = 1 - k

    def dev(y_, k_, z_, x_):
        return (y_ * 2 + k_, z_ * NX + x_)

    def remote(src, dst, send, recv, to):
        return pltpu.make_async_remote_copy(
            src_ref=src, dst_ref=dst, send_sem=send, recv_sem=recv, device_id=to, device_id_type=MESH
        )

    sends = []

    def start(copy):
        sends.append(copy)
        copy.start()

    load = pltpu.make_async_copy(blocks, held.at[pl.ds(0, slots)], load_sem)
    load.start()

    barrier = pltpu.get_barrier_semaphore()

    def greet(to):
        pl.semaphore_signal(barrier, inc=1, device_id=to, device_id_type=MESH)

    greet(dev(y, other, z, x))
    for dy in range(1, NY):
        greet(dev((y + dy) % NY, k, z, x))
    for dx in range(1, NX):
        greet(dev(y, k, z, (x + dx) % NX))
    for dz in range(1, NZ):
        greet(dev(y, k, (z + dz) % NZ, x))
    pl.semaphore_wait(barrier, NY + NX + NZ - 2)

    def g_rows(r):
        return pl.ds(pl.multiple_of(r * share, share), share)

    def g_dst(h, r):
        return gathered.at[g_rows(r), pl.ds(h * LANES, LANES)]

    for h in range(chunks):
        src = basis.at[:, pl.ds(h * LANES, LANES)]
        for dy in range(1, NY):
            start(remote(src, g_dst(h, row), g_ss.at[h, dy], g_sr.at[h, row], dev((y + dy) % NY, k, z, x)))
        start(remote(src, g_dst(h, row), g_ss.at[h, 0], g_sr.at[h, row], dev(y, other, z, x)))

    gathered[g_rows(row), :] = basis[...]

    def await_recv(dst, sem):
        remote(dst, dst, sem, sem, dev(y, other, z, x)).wait_recv()

    def gather(h):
        for dy in range(1, NY):
            r = ((y + dy) % NY) * 2 + k
            await_recv(g_dst(h, r), g_sr.at[h, r])
            start(remote(g_dst(h, r), g_dst(h, r), g_ss.at[h, NY + dy], g_sr.at[h, r], dev(y, other, z, x)))

    def gather_rest(h):
        for dy in range(NY):
            r = ((y + dy) % NY) * 2 + other
            await_recv(g_dst(h, r), g_sr.at[h, r])

    held[slots] = jnp.zeros((size, size), held.dtype)
    load.wait()

    def lay(i, _):
        for j in range(CB):
            matrix[pl.ds(pl.multiple_of(i * size, size), size), pl.ds(j * size, size)] = held[table[i * CB + j]]
        return 0

    lax.fori_loop(0, RB, lay, 0)

    def turn_all():
        def turn(s, _):
            turned[s] = held[s].T
            return 0

        lax.fori_loop(0, slots + 1, turn, 0)

    def lay_all():
        def lay_turned(j, _):
            for i in range(RB):
                flipped[pl.ds(pl.multiple_of(j * size, size), size), pl.ds(i * size, size)] = turned[table[i * CB + j]]
            return 0

        lax.fori_loop(0, CB, lay_turned, 0)

    def p_rows(x_, z_):
        return pl.ds(pl.multiple_of((x_ * NZ + z_) * piece, piece), piece)

    def x_rows(x_):
        return pl.ds(pl.multiple_of(x_ * NZ * piece, NZ * piece), NZ * piece)

    def product(x_):
        rows = x_rows(x_)
        result = jnp.dot(matrix[rows, :], gathered[...], preferred_element_type=jnp.float32)
        for h in range(chunks):
            part[h, rows, :] = result[:, h * LANES : (h + 1) * LANES]

    pairs = NZ // 2
    near = z + 1 - 2 * (z % 2)
    near_like = [(near + 2 * j) % NZ for j in range(pairs)]
    alike = [(z + 2 * j) % NZ for j in range(pairs)]
    z_order = near_like + alike[1:] + [z]

    def reduce_x(h):
        for dx in range(1, NX):
            x_ = (x + dx) % NX
            for t in z_order:
                encode(xs.at[h, dx, t], part[h, p_rows(x_, t), :])
                start(remote(xs.at[h, dx, t], xr.at[h, dx, t], x_ss.at[h, dx, t], x_sr.at[h, dx, t], dev(y, k, z, x_)))

    def add_x(h, t):
        total = part[h, p_rows(x, t), :]
        for dx in range(1, NX):
            await_recv(xr.at[h, dx, t], x_sr.at[h, dx, t])
            total = total + decode(xr.at[h, dx, t])
        return total

    def send_z(h, slot, value, to):
        encode(zs.at[h, slot], value)
        start(remote(zs.at[h, slot], zr.at[h, slot], z_ss.at[h, slot], z_sr.at[h, slot], dev(y, k, to, x)))

    def take_z(h, slot):
        await_recv(zr.at[h, slot], z_sr.at[h, slot])
        return decode(zr.at[h, slot])

    def reduce_near(h):
        for j in range(pairs):
            send_z(h, j, add_x(h, near_like[j]), near)

    def reduce_far(h):
        for j in range(1, pairs):
            send_z(h, pairs + j, add_x(h, alike[j]) + take_z(h, j), alike[j])

    def pass_x(h, t):
        ref = row_basis.at[h, p_rows(x, t)]
        for dx in range(1, NX):
            start(remote(ref, ref, ax_ss.at[h, dx, t], a_sr.at[h, x * NZ + t], dev(y, k, z, (x + dx) % NX)))

    def settle(h):
        total = add_x(h, z) + take_z(h, 0)
        for j in range(1, pairs):
            total = total + take_z(h, pairs + j)
        row_basis[h, p_rows(x, z), :] = total.astype(row_basis.dtype)
        for j in range(1, pairs):
            pass_z(h, z, j, alike[j])
        pass_z(h, z, 0, near)
        pass_x(h, z)

    def pass_z(h, t, slot, to):
        ref = row_basis.at[h, p_rows(x, t)]
        start(remote(ref, ref, az_ss.at[h, slot], a_sr.at[h, x * NZ + t], dev(y, k, to, x)))

    def arrived(h, t):
        await_recv(row_basis.at[h, p_rows(x, t)], a_sr.at[h, x * NZ + t])

    def spread_far(h):
        for j in range(1, pairs):
            arrived(h, alike[j])
            pass_z(h, alike[j], pairs + j, near)
            pass_x(h, alike[j])

    def spread_near(h, j):
        arrived(h, near_like[j])
        pass_x(h, near_like[j])

    def back_half(h, x_):
        return jnp.dot(flipped[:, x_rows(x_)], row_basis[h, x_rows(x_), :], preferred_element_type=jnp.float32)

    def back_own(h):
        part[h] = back_half(h, x)

    def collect(h):
        for dx in range(1, NX):
            x_ = (x + dx) % NX
            for t in range(NZ):
                await_recv(row_basis.at[h, p_rows(x_, t)], a_sr.at[h, x_ * NZ + t])

    def back_product(h, r):
        rows = g_rows(r)
        total = part[h, rows, :]
        for dx in range(1, NX):
            x_ = (x + dx) % NX
            total = total + jnp.dot(
                flipped[rows, x_rows(x_)], row_basis[h, x_rows(x_), :], preferred_element_type=jnp.float32
            )
        return total

    def back_core(h):
        for dy in list(range(1, NY)) + [0]:
            y_ = (y + dy) % NY
            cs[h, dy] = back_product(h, y_ * 2 + other).astype(cs.dtype)
            start(remote(cs.at[h, dy], cr.at[h, dy], c_ss.at[h, dy], c_sr.at[h, dy], dev(y, other, z, x)))

    def back_y(h):
        for dy in list(range(1, NY)) + [0]:
            y_ = (y + dy) % NY
            total = back_product(h, y_ * 2 + k)
            await_recv(cr.at[h, dy], c_sr.at[h, dy])
            total = total + cr[h, dy].astype(jnp.float32)
            if dy > 0:
                ys[h, dy] = total.astype(ys.dtype)
                start(remote(ys.at[h, dy], yr.at[h, dy], y_ss.at[h, dy], y_sr.at[h, dy], dev(y_, k, z, x)))
            else:
                out[:, pl.ds(h * LANES, LANES)] = total

    def finish(h):
        total = out[:, pl.ds(h * LANES, LANES)]
        for dy in range(1, NY):
            await_recv(yr.at[h, dy], y_sr.at[h, dy])
            total = total + yr[h, dy].astype(jnp.float32)
        out[:, pl.ds(h * LANES, LANES)] = total

    turn_all()
    for h in range(chunks):
        gather(h)
    for h in range(chunks):
        gather_rest(h)
    for dx in range(1, NX):
        product((x + dx) % NX)
    for h in range(chunks):
        reduce_x(h)
    product(x)
    for h in range(chunks):
        reduce_near(h)
        if h == 0:
            lay_all()
        else:
            spread_far(h - 1)
        reduce_far(h)
        if h > 0:
            for j in range(pairs):
                spread_near(h - 1, j)
        settle(h)
        if h > 0:
            back_own(h - 1)
    last = chunks - 1
    spread_far(last)
    spread_near(last, 0)
    for h in range(last):
        collect(h)
        back_core(h)
    for j in range(1, pairs):
        spread_near(last, j)
    for h in range(last):
        back_y(h)
    back_own(last)
    collect(last)
    back_core(last)
    back_y(last)
    for h in range(chunks):
        finish(h)
    for copy in sends:
        copy.wait_send()


def body(NR, NC, block_values, block_rows, block_cols, block_count, basis):
    blocks = block_values[0, 0]
    slots, size, _ = blocks.shape
    share, rank = basis.shape
    NX = math.isqrt(max(NC // 2, 1))
    if NC % NX:
        NX = 1
    NZ = NC // NX
    NY = NR // 2
    chunks = rank // LANES
    piece = RB * size // NC
    places = jnp.where(
        jnp.arange(slots, dtype=jnp.int32) < block_count[0, 0], block_rows[0, 0] * CB + block_cols[0, 0], -1
    )
    hit = places[None, :] == jnp.arange(RB * CB, dtype=jnp.int32)[:, None]
    table = jnp.min(jnp.where(hit, jnp.arange(slots, dtype=jnp.int32)[None, :], slots), axis=1)
    bf16, i16 = jnp.bfloat16, jnp.int16
    DMA = pltpu.SemaphoreType.DMA
    V = pltpu.VMEM
    return pl.pallas_call(
        functools.partial(kernel, NR, NX, NZ),
        out_shape=jax.ShapeDtypeStruct((share, rank), jnp.float32),
        in_specs=[
            pl.BlockSpec(memory_space=pltpu.SMEM),
            pl.BlockSpec(memory_space=pltpu.VMEM),
            pl.BlockSpec(memory_space=pl.ANY),
        ],
        out_specs=pl.BlockSpec(memory_space=pltpu.VMEM),
        scratch_shapes=[
            V((slots + 1, size, size), bf16),
            V((slots + 1, size, size), bf16),
            V((RB * size, CB * size), bf16),
            V((CB * size, RB * size), bf16),
            V((CB * size, rank), bf16),
            V((chunks, RB * size, LANES), jnp.float32),
            V((chunks, NX, NZ, piece + EXTRA, LANES), i16),
            V((chunks, NX, NZ, piece + EXTRA, LANES), i16),
            V((chunks, NZ, piece + EXTRA, LANES), i16),
            V((chunks, NZ, piece + EXTRA, LANES), i16),
            V((chunks, RB * size, LANES), bf16),
            V((chunks, NY, share, LANES), bf16),
            V((chunks, NY, share, LANES), bf16),
            V((chunks, NY, share, LANES), bf16),
            V((chunks, NY, share, LANES), bf16),
            DMA,
            DMA((chunks, 2 * NY)),
            DMA((chunks, NR)),
            DMA((chunks, NX, NZ)),
            DMA((chunks, NX, NZ)),
            DMA((chunks, NZ)),
            DMA((chunks, NZ)),
            DMA((chunks, NZ)),
            DMA((chunks, NX, NZ)),
            DMA((chunks, NC)),
            DMA((chunks, NY)),
            DMA((chunks, NY)),
            DMA((chunks, NY)),
            DMA((chunks, NY)),
        ],
        compiler_params=pltpu.CompilerParams(
            collective_id=0, has_side_effects=True, vmem_limit_bytes=56 * 1024 * 1024
        ),
    )(table, basis, blocks)


def solution(mesh):
    in_specs = (
        P("row", "col", None, None, None),
        P("row", "col", None),
        P("row", "col", None),
        P("row", "col"),
        P(("col", "row"), None),
    )
    out_specs = P(("col", "row"), None)
    run = functools.partial(body, mesh.shape["row"], mesh.shape["col"])
    return jax.shard_map(run, mesh=mesh, in_specs=in_specs, out_specs=out_specs, check_vma=False)
```

```python
import functools
import math

import jax
import jax.numpy as jnp
from jax import lax
from jax.experimental import pallas as pl
from jax.experimental.pallas import tpu as pltpu
from jax.sharding import PartitionSpec as P

RB = 8
CB = 8
LANES = 128
EXTRA = 16
MESH = pl.DeviceIdType.MESH


def encode(dst, value):
    rows = value.shape[0]
    top = jnp.max(jnp.abs(value), axis=0, keepdims=True)
    power = jnp.floor(jnp.log2(jnp.maximum(top, 1e-30)))
    scaled = jnp.round(value * jnp.exp2(13.9 - power)).astype(jnp.int32)
    dst[pl.ds(0, rows), :] = scaled.astype(jnp.int16)
    tail = jnp.broadcast_to(power.astype(jnp.int32), (EXTRA, value.shape[1]))
    dst[pl.ds(rows, EXTRA), :] = tail.astype(jnp.int16)


def decode(src):
    rows = src.shape[0] - EXTRA
    power = src[pl.ds(rows, EXTRA), :].astype(jnp.int32).astype(jnp.float32)[0:1, :]
    values = src[pl.ds(0, rows), :].astype(jnp.int32).astype(jnp.float32)
    return values * jnp.exp2(power - 13.9)


def kernel(
    NR, NX, NZ,
    table, basis, blocks, out,
    held, turned, matrix, flipped, gathered, part, xs, xr, zs, zr, row_basis, cs, cr, ys, yr,
    load_sem, g_ss, g_sr, x_ss, x_sr, z_ss, z_sr, az_ss, ax_ss, a_sr, c_ss, c_sr, y_ss, y_sr,
):
    NY = NR // 2
    slots, size, _ = blocks.shape
    chunks = part.shape[0]
    share = basis.shape[0]
    piece = part.shape[1] // (NX * NZ)
    row = lax.axis_index("row")
    col = lax.axis_index("col")
    y, k = row // 2, row % 2
    z, x = col // NX, col % NX
    other = 1 - k

    def dev(y_, k_, z_, x_):
        return (y_ * 2 + k_, z_ * NX + x_)

    def remote(src, dst, send, recv, to):
        return pltpu.make_async_remote_copy(
            src_ref=src, dst_ref=dst, send_sem=send, recv_sem=recv, device_id=to, device_id_type=MESH
        )

    sends = []

    def start(copy):
        sends.append(copy)
        copy.start()

    load = pltpu.make_async_copy(blocks, held.at[pl.ds(0, slots)], load_sem)
    load.start()

    barrier = pltpu.get_barrier_semaphore()

    def greet(to):
        pl.semaphore_signal(barrier, inc=1, device_id=to, device_id_type=MESH)

    greet(dev(y, other, z, x))
    for dy in range(1, NY):
        greet(dev((y + dy) % NY, k, z, x))
    for dx in range(1, NX):
        greet(dev(y, k, z, (x + dx) % NX))
    for dz in range(1, NZ):
        greet(dev(y, k, (z + dz) % NZ, x))
    pl.semaphore_wait(barrier, NY + NX + NZ - 2)

    def g_rows(r):
        return pl.ds(pl.multiple_of(r * share, share), share)

    def g_dst(h, r):
        return gathered.at[g_rows(r), pl.ds(h * LANES, LANES)]

    for h in range(chunks):
        src = basis.at[:, pl.ds(h * LANES, LANES)]
        for dy in range(1, NY):
            start(remote(src, g_dst(h, row), g_ss.at[h, dy], g_sr.at[h, row], dev((y + dy) % NY, k, z, x)))
        start(remote(src, g_dst(h, row), g_ss.at[h, 0], g_sr.at[h, row], dev(y, other, z, x)))

    gathered[g_rows(row), :] = basis[...]

    def await_recv(dst, sem):
        remote(dst, dst, sem, sem, dev(y, other, z, x)).wait_recv()

    def gather(h):
        for dy in range(1, NY):
            r = ((y + dy) % NY) * 2 + k
            await_recv(g_dst(h, r), g_sr.at[h, r])
            start(remote(g_dst(h, r), g_dst(h, r), g_ss.at[h, NY + dy], g_sr.at[h, r], dev(y, other, z, x)))

    def gather_rest(h):
        for dy in range(NY):
            r = ((y + dy) % NY) * 2 + other
            await_recv(g_dst(h, r), g_sr.at[h, r])

    held[slots] = jnp.zeros((size, size), held.dtype)
    load.wait()

    def lay(i, _):
        for j in range(CB):
            matrix[pl.ds(pl.multiple_of(i * size, size), size), pl.ds(j * size, size)] = held[table[i * CB + j]]
        return 0

    lax.fori_loop(0, RB, lay, 0)

    def turn_all():
        def turn(s, _):
            turned[s] = held[s].T
            return 0

        lax.fori_loop(0, slots + 1, turn, 0)

    def lay_all():
        def lay_turned(j, _):
            for i in range(RB):
                flipped[pl.ds(pl.multiple_of(j * size, size), size), pl.ds(i * size, size)] = turned[table[i * CB + j]]
            return 0

        lax.fori_loop(0, CB, lay_turned, 0)

    def p_rows(x_, z_):
        return pl.ds(pl.multiple_of((x_ * NZ + z_) * piece, piece), piece)

    def x_rows(x_):
        return pl.ds(pl.multiple_of(x_ * NZ * piece, NZ * piece), NZ * piece)

    def product(x_):
        rows = x_rows(x_)
        result = jnp.dot(matrix[rows, :], gathered[...], preferred_element_type=jnp.float32)
        for h in range(chunks):
            part[h, rows, :] = result[:, h * LANES : (h + 1) * LANES]

    z_order = [(z + dz) % NZ for dz in range(1, NZ)]

    def reduce_x(h):
        for dx in range(1, NX):
            x_ = (x + dx) % NX
            for t in z_order + [z]:
                encode(xs.at[h, dx, t], part[h, p_rows(x_, t), :])
                start(remote(xs.at[h, dx, t], xr.at[h, dx, t], x_ss.at[h, dx, t], x_sr.at[h, dx, t], dev(y, k, z, x_)))

    def add_x(h, t):
        total = part[h, p_rows(x, t), :]
        for dx in range(1, NX):
            await_recv(xr.at[h, dx, t], x_sr.at[h, dx, t])
            total = total + decode(xr.at[h, dx, t])
        return total

    def reduce_z(h):
        for dz, t in enumerate(z_order, 1):
            encode(zs.at[h, dz], add_x(h, t))
            start(remote(zs.at[h, dz], zr.at[h, dz], z_ss.at[h, dz], z_sr.at[h, dz], dev(y, k, t, x)))

    def pass_x(h, t):
        ref = row_basis.at[h, p_rows(x, t)]
        for dx in range(1, NX):
            start(remote(ref, ref, ax_ss.at[h, dx, t], a_sr.at[h, x * NZ + t], dev(y, k, z, (x + dx) % NX)))

    def settle(h):
        total = add_x(h, z)
        for dz in range(1, NZ):
            await_recv(zr.at[h, dz], z_sr.at[h, dz])
            total = total + decode(zr.at[h, dz])
        row_basis[h, p_rows(x, z), :] = total.astype(row_basis.dtype)
        ref = row_basis.at[h, p_rows(x, z)]
        for dz, t in enumerate(z_order, 1):
            start(remote(ref, ref, az_ss.at[h, dz], a_sr.at[h, x * NZ + z], dev(y, k, t, x)))
        pass_x(h, z)

    def spread(h, order):
        for t in order:
            await_recv(row_basis.at[h, p_rows(x, t)], a_sr.at[h, x * NZ + t])
            pass_x(h, t)

    def back_half(h, x_):
        return jnp.dot(flipped[:, x_rows(x_)], row_basis[h, x_rows(x_), :], preferred_element_type=jnp.float32)

    def back_own(h):
        part[h] = back_half(h, x)

    def collect(h):
        for dx in range(1, NX):
            x_ = (x + dx) % NX
            for t in range(NZ):
                await_recv(row_basis.at[h, p_rows(x_, t)], a_sr.at[h, x_ * NZ + t])

    def back_product(h, r):
        rows = g_rows(r)
        total = part[h, rows, :]
        for dx in range(1, NX):
            x_ = (x + dx) % NX
            total = total + jnp.dot(
                flipped[rows, x_rows(x_)], row_basis[h, x_rows(x_), :], preferred_element_type=jnp.float32
            )
        return total

    def back_core(h):
        for dy in list(range(1, NY)) + [0]:
            y_ = (y + dy) % NY
            cs[h, dy] = back_product(h, y_ * 2 + other).astype(cs.dtype)
            start(remote(cs.at[h, dy], cr.at[h, dy], c_ss.at[h, dy], c_sr.at[h, dy], dev(y, other, z, x)))

    def back_y(h):
        for dy in list(range(1, NY)) + [0]:
            y_ = (y + dy) % NY
            total = back_product(h, y_ * 2 + k)
            await_recv(cr.at[h, dy], c_sr.at[h, dy])
            total = total + cr[h, dy].astype(jnp.float32)
            if dy > 0:
                ys[h, dy] = total.astype(ys.dtype)
                start(remote(ys.at[h, dy], yr.at[h, dy], y_ss.at[h, dy], y_sr.at[h, dy], dev(y_, k, z, x)))
            else:
                out[:, pl.ds(h * LANES, LANES)] = total

    def finish(h):
        total = out[:, pl.ds(h * LANES, LANES)]
        for dy in range(1, NY):
            await_recv(yr.at[h, dy], y_sr.at[h, dy])
            total = total + yr[h, dy].astype(jnp.float32)
        out[:, pl.ds(h * LANES, LANES)] = total

    turn_all()
    for h in range(chunks):
        gather(h)
    for h in range(chunks):
        gather_rest(h)
    for dx in range(1, NX):
        product((x + dx) % NX)
    for h in range(chunks):
        reduce_x(h)
    product(x)
    for h in range(chunks - 1):
        reduce_z(h)
        if h == 0:
            lay_all()
        settle(h)
        if h > 0:
            spread(h - 1, z_order)
            back_own(h - 1)
    if chunks == 1:
        lay_all()
    last = chunks - 1
    reduce_z(last)
    if last > 0:
        spread(last - 1, z_order)
    settle(last)
    if last > 0:
        back_own(last - 1)
    spread(last, z_order[:1])
    for h in range(last):
        collect(h)
        back_core(h)
    spread(last, z_order[1:])
    for h in range(last):
        back_y(h)
    back_own(last)
    collect(last)
    back_core(last)
    back_y(last)
    for h in range(chunks):
        finish(h)
    for copy in sends:
        copy.wait_send()


def body(NR, NC, block_values, block_rows, block_cols, block_count, basis):
    blocks = block_values[0, 0]
    slots, size, _ = blocks.shape
    share, rank = basis.shape
    NX = math.isqrt(max(NC // 2, 1))
    if NC % NX:
        NX = 1
    NZ = NC // NX
    NY = NR // 2
    chunks = rank // LANES
    piece = RB * size // NC
    places = jnp.where(
        jnp.arange(slots, dtype=jnp.int32) < block_count[0, 0], block_rows[0, 0] * CB + block_cols[0, 0], -1
    )
    hit = places[None, :] == jnp.arange(RB * CB, dtype=jnp.int32)[:, None]
    table = jnp.min(jnp.where(hit, jnp.arange(slots, dtype=jnp.int32)[None, :], slots), axis=1)
    bf16, i16 = jnp.bfloat16, jnp.int16
    DMA = pltpu.SemaphoreType.DMA
    V = pltpu.VMEM
    return pl.pallas_call(
        functools.partial(kernel, NR, NX, NZ),
        out_shape=jax.ShapeDtypeStruct((share, rank), jnp.float32),
        in_specs=[
            pl.BlockSpec(memory_space=pltpu.SMEM),
            pl.BlockSpec(memory_space=pltpu.VMEM),
            pl.BlockSpec(memory_space=pl.ANY),
        ],
        out_specs=pl.BlockSpec(memory_space=pltpu.VMEM),
        scratch_shapes=[
            V((slots + 1, size, size), bf16),
            V((slots + 1, size, size), bf16),
            V((RB * size, CB * size), bf16),
            V((CB * size, RB * size), bf16),
            V((CB * size, rank), bf16),
            V((chunks, RB * size, LANES), jnp.float32),
            V((chunks, NX, NZ, piece + EXTRA, LANES), i16),
            V((chunks, NX, NZ, piece + EXTRA, LANES), i16),
            V((chunks, NZ, piece + EXTRA, LANES), i16),
            V((chunks, NZ, piece + EXTRA, LANES), i16),
            V((chunks, RB * size, LANES), bf16),
            V((chunks, NY, share, LANES), bf16),
            V((chunks, NY, share, LANES), bf16),
            V((chunks, NY, share, LANES), bf16),
            V((chunks, NY, share, LANES), bf16),
            DMA,
            DMA((chunks, 2 * NY)),
            DMA((chunks, NR)),
            DMA((chunks, NX, NZ)),
            DMA((chunks, NX, NZ)),
            DMA((chunks, NZ)),
            DMA((chunks, NZ)),
            DMA((chunks, NZ)),
            DMA((chunks, NX, NZ)),
            DMA((chunks, NC)),
            DMA((chunks, NY)),
            DMA((chunks, NY)),
            DMA((chunks, NY)),
            DMA((chunks, NY)),
        ],
        compiler_params=pltpu.CompilerParams(
            collective_id=0, has_side_effects=True, vmem_limit_bytes=56 * 1024 * 1024
        ),
    )(table, basis, blocks)


def solution(mesh):
    in_specs = (
        P("row", "col", None, None, None),
        P("row", "col", None),
        P("row", "col", None),
        P("row", "col"),
        P(("col", "row"), None),
    )
    out_specs = P(("col", "row"), None)
    run = functools.partial(body, mesh.shape["row"], mesh.shape["col"])
    return jax.shard_map(run, mesh=mesh, in_specs=in_specs, out_specs=out_specs, check_vma=False)
```

```python
import functools
import math

import jax
import jax.numpy as jnp
from jax import lax
from jax.experimental import pallas as pl
from jax.experimental.pallas import tpu as pltpu
from jax.sharding import PartitionSpec as P

RB = 8
CB = 8
LANES = 128
EXTRA = 16
MESH = pl.DeviceIdType.MESH


def encode(dst, value):
    rows = value.shape[0]
    top = jnp.max(jnp.abs(value), axis=0, keepdims=True)
    power = jnp.floor(jnp.log2(jnp.maximum(top, 1e-30)))
    scaled = jnp.round(value * jnp.exp2(13.9 - power)).astype(jnp.int32)
    dst[pl.ds(0, rows), :] = scaled.astype(jnp.int16)
    tail = jnp.broadcast_to(power.astype(jnp.int32), (EXTRA, value.shape[1]))
    dst[pl.ds(rows, EXTRA), :] = tail.astype(jnp.int16)


def decode(src):
    rows = src.shape[0] - EXTRA
    power = src[pl.ds(rows, EXTRA), :].astype(jnp.int32).astype(jnp.float32)[0:1, :]
    values = src[pl.ds(0, rows), :].astype(jnp.int32).astype(jnp.float32)
    return values * jnp.exp2(power - 13.9)


def kernel(
    NR, NX, NZ,
    table, basis, blocks, out,
    held, turned, matrix, flipped, gathered, part, xs, xr, zs, zr, row_basis, cs, cr, ys, yr,
    load_sem, g_ss, g_sr, x_ss, x_sr, z_ss, z_sr, az_ss, ax_ss, a_sr, c_ss, c_sr, y_ss, y_sr,
):
    NY = NR // 2
    slots, size, _ = blocks.shape
    chunks = part.shape[0]
    share = basis.shape[0]
    piece = part.shape[1] // (NX * NZ)
    row = lax.axis_index("row")
    col = lax.axis_index("col")
    y, k = row // 2, row % 2
    z, x = col // NX, col % NX
    other = 1 - k

    def dev(y_, k_, z_, x_):
        return (y_ * 2 + k_, z_ * NX + x_)

    def remote(src, dst, send, recv, to):
        return pltpu.make_async_remote_copy(
            src_ref=src, dst_ref=dst, send_sem=send, recv_sem=recv, device_id=to, device_id_type=MESH
        )

    sends = []

    def start(copy):
        sends.append(copy)
        copy.start()

    load = pltpu.make_async_copy(blocks, held.at[pl.ds(0, slots)], load_sem)
    load.start()

    barrier = pltpu.get_barrier_semaphore()

    def greet(to):
        pl.semaphore_signal(barrier, inc=1, device_id=to, device_id_type=MESH)

    greet(dev(y, other, z, x))
    for dy in range(1, NY):
        greet(dev((y + dy) % NY, k, z, x))
    for dx in range(1, NX):
        greet(dev(y, k, z, (x + dx) % NX))
    for dz in range(1, NZ):
        greet(dev(y, k, (z + dz) % NZ, x))
    pl.semaphore_wait(barrier, NY + NX + NZ - 2)

    def g_rows(r):
        return pl.ds(pl.multiple_of(r * share, share), share)

    def g_dst(h, r):
        return gathered.at[g_rows(r), pl.ds(h * LANES, LANES)]

    for h in range(chunks):
        src = basis.at[:, pl.ds(h * LANES, LANES)]
        for dy in range(1, NY):
            start(remote(src, g_dst(h, row), g_ss.at[h, dy], g_sr.at[h, row], dev((y + dy) % NY, k, z, x)))
        start(remote(src, g_dst(h, row), g_ss.at[h, 0], g_sr.at[h, row], dev(y, other, z, x)))

    gathered[g_rows(row), :] = basis[...]

    def await_recv(dst, sem):
        remote(dst, dst, sem, sem, dev(y, other, z, x)).wait_recv()

    def gather(h):
        for dy in range(1, NY):
            r = ((y + dy) % NY) * 2 + k
            await_recv(g_dst(h, r), g_sr.at[h, r])
            start(remote(g_dst(h, r), g_dst(h, r), g_ss.at[h, NY + dy], g_sr.at[h, r], dev(y, other, z, x)))

    def gather_rest(h):
        for dy in range(NY):
            r = ((y + dy) % NY) * 2 + other
            await_recv(g_dst(h, r), g_sr.at[h, r])

    held[slots] = jnp.zeros((size, size), held.dtype)
    load.wait()

    def lay(i, _):
        for j in range(CB):
            matrix[pl.ds(pl.multiple_of(i * size, size), size), pl.ds(j * size, size)] = held[table[i * CB + j]]
        return 0

    lax.fori_loop(0, RB, lay, 0)

    def turn_some(first, last):
        def turn(s, _):
            turned[s] = held[s].T
            return 0

        lax.fori_loop(first, last, turn, 0)

    def lay_all():
        def lay_turned(j, _):
            for i in range(RB):
                flipped[pl.ds(pl.multiple_of(j * size, size), size), pl.ds(i * size, size)] = turned[table[i * CB + j]]
            return 0

        lax.fori_loop(0, CB, lay_turned, 0)

    def p_rows(x_, z_):
        return pl.ds(pl.multiple_of((x_ * NZ + z_) * piece, piece), piece)

    def x_rows(x_):
        return pl.ds(pl.multiple_of(x_ * NZ * piece, NZ * piece), NZ * piece)

    def product(x_):
        rows = x_rows(x_)
        result = jnp.dot(matrix[rows, :], gathered[...], preferred_element_type=jnp.float32)
        for h in range(chunks):
            part[h, rows, :] = result[:, h * LANES : (h + 1) * LANES]

    z_order = [(z + dz) % NZ for dz in range(1, NZ)]

    def reduce_x(h):
        for dx in range(1, NX):
            x_ = (x + dx) % NX
            for t in z_order + [z]:
                encode(xs.at[h, dx, t], part[h, p_rows(x_, t), :])
                start(remote(xs.at[h, dx, t], xr.at[h, dx, t], x_ss.at[h, dx, t], x_sr.at[h, dx, t], dev(y, k, z, x_)))

    def add_x(h, t):
        total = part[h, p_rows(x, t), :]
        for dx in range(1, NX):
            await_recv(xr.at[h, dx, t], x_sr.at[h, dx, t])
            total = total + decode(xr.at[h, dx, t])
        return total

    def reduce_z(h):
        for dz, t in enumerate(z_order, 1):
            encode(zs.at[h, dz], add_x(h, t))
            start(remote(zs.at[h, dz], zr.at[h, dz], z_ss.at[h, dz], z_sr.at[h, dz], dev(y, k, t, x)))

    def pass_x(h, t):
        ref = row_basis.at[h, p_rows(x, t)]
        for dx in range(1, NX):
            start(remote(ref, ref, ax_ss.at[h, dx, t], a_sr.at[h, x * NZ + t], dev(y, k, z, (x + dx) % NX)))

    def settle(h):
        total = add_x(h, z)
        for dz in range(1, NZ):
            await_recv(zr.at[h, dz], z_sr.at[h, dz])
            total = total + decode(zr.at[h, dz])
        row_basis[h, p_rows(x, z), :] = total.astype(row_basis.dtype)
        ref = row_basis.at[h, p_rows(x, z)]
        for dz, t in enumerate(z_order, 1):
            start(remote(ref, ref, az_ss.at[h, dz], a_sr.at[h, x * NZ + z], dev(y, k, t, x)))
        pass_x(h, z)

    def spread(h, order):
        for t in order:
            await_recv(row_basis.at[h, p_rows(x, t)], a_sr.at[h, x * NZ + t])
            pass_x(h, t)

    def back_half(h, x_):
        return jnp.dot(flipped[:, x_rows(x_)], row_basis[h, x_rows(x_), :], preferred_element_type=jnp.float32)

    def back_own(h):
        part[h] = back_half(h, x)

    def collect(h):
        for dx in range(1, NX):
            x_ = (x + dx) % NX
            for t in range(NZ):
                await_recv(row_basis.at[h, p_rows(x_, t)], a_sr.at[h, x_ * NZ + t])

    def back_product(h, r):
        rows = g_rows(r)
        total = part[h, rows, :]
        for dx in range(1, NX):
            x_ = (x + dx) % NX
            total = total + jnp.dot(
                flipped[rows, x_rows(x_)], row_basis[h, x_rows(x_), :], preferred_element_type=jnp.float32
            )
        return total

    def back_core(h):
        for dy in list(range(1, NY)) + [0]:
            y_ = (y + dy) % NY
            cs[h, dy] = back_product(h, y_ * 2 + other).astype(cs.dtype)
            start(remote(cs.at[h, dy], cr.at[h, dy], c_ss.at[h, dy], c_sr.at[h, dy], dev(y, other, z, x)))

    def back_y(h):
        for dy in list(range(1, NY)) + [0]:
            y_ = (y + dy) % NY
            total = back_product(h, y_ * 2 + k)
            await_recv(cr.at[h, dy], c_sr.at[h, dy])
            total = total + cr[h, dy].astype(jnp.float32)
            if dy > 0:
                ys[h, dy] = total.astype(ys.dtype)
                start(remote(ys.at[h, dy], yr.at[h, dy], y_ss.at[h, dy], y_sr.at[h, dy], dev(y_, k, z, x)))
            else:
                out[:, pl.ds(h * LANES, LANES)] = total

    def finish(h):
        total = out[:, pl.ds(h * LANES, LANES)]
        for dy in range(1, NY):
            await_recv(yr.at[h, dy], y_sr.at[h, dy])
            total = total + yr[h, dy].astype(jnp.float32)
        out[:, pl.ds(h * LANES, LANES)] = total

    turn_some(0, slots // 2)
    for h in range(chunks):
        gather(h)
    for h in range(chunks):
        gather_rest(h)
    for dx in range(1, NX):
        product((x + dx) % NX)
    for h in range(chunks):
        reduce_x(h)
    product(x)
    for h in range(chunks - 1):
        reduce_z(h)
        if h == 0:
            turn_some(slots // 2, slots + 1)
            lay_all()
        settle(h)
        if h > 0:
            spread(h - 1, z_order)
            back_own(h - 1)
    if chunks == 1:
        turn_some(slots // 2, slots + 1)
        lay_all()
    last = chunks - 1
    reduce_z(last)
    if last > 0:
        spread(last - 1, z_order)
    settle(last)
    if last > 0:
        back_own(last - 1)
    spread(last, z_order[:1])
    for h in range(last):
        collect(h)
        back_core(h)
    spread(last, z_order[1:])
    for h in range(last):
        back_y(h)
    back_own(last)
    collect(last)
    back_core(last)
    back_y(last)
    for h in range(chunks):
        finish(h)
    for copy in sends:
        copy.wait_send()


def body(NR, NC, block_values, block_rows, block_cols, block_count, basis):
    blocks = block_values[0, 0]
    slots, size, _ = blocks.shape
    share, rank = basis.shape
    NX = math.isqrt(max(NC // 2, 1))
    if NC % NX:
        NX = 1
    NZ = NC // NX
    NY = NR // 2
    chunks = rank // LANES
    piece = RB * size // NC
    places = jnp.where(
        jnp.arange(slots, dtype=jnp.int32) < block_count[0, 0], block_rows[0, 0] * CB + block_cols[0, 0], -1
    )
    hit = places[None, :] == jnp.arange(RB * CB, dtype=jnp.int32)[:, None]
    table = jnp.min(jnp.where(hit, jnp.arange(slots, dtype=jnp.int32)[None, :], slots), axis=1)
    bf16, i16 = jnp.bfloat16, jnp.int16
    DMA = pltpu.SemaphoreType.DMA
    V = pltpu.VMEM
    return pl.pallas_call(
        functools.partial(kernel, NR, NX, NZ),
        out_shape=jax.ShapeDtypeStruct((share, rank), jnp.float32),
        in_specs=[
            pl.BlockSpec(memory_space=pltpu.SMEM),
            pl.BlockSpec(memory_space=pltpu.VMEM),
            pl.BlockSpec(memory_space=pl.ANY),
        ],
        out_specs=pl.BlockSpec(memory_space=pltpu.VMEM),
        scratch_shapes=[
            V((slots + 1, size, size), bf16),
            V((slots + 1, size, size), bf16),
            V((RB * size, CB * size), bf16),
            V((CB * size, RB * size), bf16),
            V((CB * size, rank), bf16),
            V((chunks, RB * size, LANES), jnp.float32),
            V((chunks, NX, NZ, piece + EXTRA, LANES), i16),
            V((chunks, NX, NZ, piece + EXTRA, LANES), i16),
            V((chunks, NZ, piece + EXTRA, LANES), i16),
            V((chunks, NZ, piece + EXTRA, LANES), i16),
            V((chunks, RB * size, LANES), bf16),
            V((chunks, NY, share, LANES), bf16),
            V((chunks, NY, share, LANES), bf16),
            V((chunks, NY, share, LANES), bf16),
            V((chunks, NY, share, LANES), bf16),
            DMA,
            DMA((chunks, 2 * NY)),
            DMA((chunks, NR)),
            DMA((chunks, NX, NZ)),
            DMA((chunks, NX, NZ)),
            DMA((chunks, NZ)),
            DMA((chunks, NZ)),
            DMA((chunks, NZ)),
            DMA((chunks, NX, NZ)),
            DMA((chunks, NC)),
            DMA((chunks, NY)),
            DMA((chunks, NY)),
            DMA((chunks, NY)),
            DMA((chunks, NY)),
        ],
        compiler_params=pltpu.CompilerParams(
            collective_id=0, has_side_effects=True, vmem_limit_bytes=56 * 1024 * 1024
        ),
    )(table, basis, blocks)


def solution(mesh):
    in_specs = (
        P("row", "col", None, None, None),
        P("row", "col", None),
        P("row", "col", None),
        P("row", "col"),
        P(("col", "row"), None),
    )
    out_specs = P(("col", "row"), None)
    run = functools.partial(body, mesh.shape["row"], mesh.shape["col"])
    return jax.shard_map(run, mesh=mesh, in_specs=in_specs, out_specs=out_specs, check_vma=False)
```
